32 devices in a mesh: expert: 4 (over z), zero: 8 (over y, x, core).
Axes of the slice: x: 2, y: 2, z: 4, core: 2. Of those that a mesh axis runs over, the one named last changes fastest.
Arguments:
- tokens: bfloat16 [4096, 2048], P(('expert', 'zero')), may hold values from -6 to 6
- router_weight: bfloat16 [2048, 32], P('zero'), may hold values from -0.25 to 0.25
- expert_ids: int32 [4096, 8], P(('expert', 'zero')), may hold values from 0 to 31, all different within a row; in each aligned block of 128 rows (0 to 127, 128 to 255, ...) at most 40 rows name the same one
- gate_weight: bfloat16 [32, 2048, 768], P(('expert', 'zero')), may hold values from -0.125 to 0.125
- up_weight: bfloat16 [32, 2048, 768], P(('expert', 'zero')), may hold values from -0.125 to 0.125
- down_weight: bfloat16 [32, 768, 2048], P(('expert', 'zero')), may hold values from -0.21875 to 0.21875
Outputs:
- mixed: bfloat16 [4096, 2048], P(('expert', 'zero'))
The draws below stay inside these ranges and needn't reach their ends.
Inputs may be any that keep to these rules, and one draw needn't show every extreme that they name: `expert_ids`: among the rows of one device no expert is named by more than 40 rows, a bound that some block reaches.
All inputs are finite; a program needn't handle non-finite values.
Results may differ from the reference program's by a relative error of at most 0.0057.
Values may be sent and summed in bfloat16 or wider, within the bound.
No kernel may reach another device: no remote copies, remote signals or barrier semaphores. Data moves between devices by JAX's collectives and lax.ppermute only.
A program may use at most 128 MiB of HBM per device.

```python
import math
import jax
import jax.numpy as jnp
import numpy as np
from jax import lax

D = 2048
FF = 768
TOPK = 8
TOK_DEV = 128
EXPERTS = 32
TOKENS = 4096
CAP = 40


def shard_levels(stream_key, shape, split, smallest, high):
    level, own = 1.0, jax.random.fold_in(stream_key, 6)
    for dim, parts in split:
        heights = jnp.exp(jax.random.uniform(jax.random.fold_in(own, dim), (parts,), jnp.float32, smallest / len(split), high / len(split)))
        level = level * jnp.repeat(heights, shape[dim] // parts).reshape([-1 if axis == dim else 1 for axis in range(len(shape))])
    return level


def deal_out(own_key, own, number, rows, amount, top, reach, skew):
    order = jax.random.permutation(own_key, amount)
    heavy_load, common = load_shares(amount, rows * top, reach, skew, True), load_shares(amount, rows * top, reach, skew, False)
    places = jnp.arange(amount)

    def named(sizes, rotation):
        used = int((sizes > 0).sum())
        fixed = max(1, used // 4)
        moved = fixed + (places - fixed + rotation * (used - fixed)) % max(1, amount - fixed)
        return jnp.zeros((amount,), jnp.int32).at[order[jnp.where(places < fixed, places, moved)]].set(jnp.asarray(sizes, jnp.int32))

    sizes = jnp.where(number % 4 == 0, named(heavy_load, number // 4), named(common, number - number // 4 - 1))
    mixed = jax.random.permutation(jax.random.fold_in(own, 3), amount)
    source_of, taker = mixed[0:amount // 2 * 2:2], mixed[1:amount // 2 * 2:2]
    margin = jnp.minimum(sizes[source_of] - 1, reach - sizes[taker]) // 2
    margin = jnp.where((source_of == order[0]) | (taker == order[0]) | (sizes[taker] == 0), 0, jnp.maximum(margin, 0))
    moved = jax.random.randint(jax.random.fold_in(own, 4), (amount // 2,), 0, 1 << 20) % (margin + 1)
    sizes = sizes.at[source_of].add(-moved).at[taker].add(moved)
    labels = jnp.searchsorted(jnp.cumsum(sizes), jnp.arange(rows * top), side="right").astype(jnp.int32)
    grid = labels.reshape(top, rows).T
    grid = grid[jax.random.permutation(jax.random.fold_in(own, 1), rows)]
    rotation = jax.random.randint(jax.random.fold_in(own, 2), (rows, 1), 0, top)
    return jnp.take_along_axis(grid, (jnp.arange(top)[None, :] + rotation) % top, axis=1)


def load_shares(amount, total, limit, slope, full):
    loads = [(1 << 20) // math.isqrt(grade ** slope) + 1 for grade in range(1, amount + 1)]
    largest = limit if full else min(limit, max(-(-total // amount), total * loads[0] // sum(loads)))
    least = 1 if total - largest >= amount - 1 else 0
    counts, surplus = [largest] + [least] * (amount - 1), total - largest - least * (amount - 1)
    while surplus > 0:
        candidates = [i for i in range(1, amount) if counts[i] < largest] or [i for i in range(1, amount) if counts[i] < limit]
        mass, budget = sum([loads[i] for i in candidates]), surplus
        for i in candidates:
            addition = min(limit - counts[i], max(1, budget * loads[i] // mass), surplus)
            counts[i] = counts[i] + addition
            surplus = surplus - addition
    return np.array(counts)


def centred(rng, extent, spread, most, shards=(), kind=jnp.bfloat16):
    level = shard_levels(rng, extent, shards, -0.22, 0.18) if shards else 1.0
    values = jax.random.normal(rng, extent, jnp.float32) * spread * level
    return jnp.minimum(jnp.maximum(values, -most), most).astype(kind)


def setup_inputs(seed: int = 0) -> dict:
    seeds = jax.random.split(jax.random.key(seed), 7)
    tokens = centred(seeds[0], (TOKENS, D), 1.0, 6.0, ((0, 32),))
    router_weight = centred(seeds[1], (D, EXPERTS), (D // 4) ** -0.5, 0.25, ((0, 8),))
    expert_ids_keys = jax.random.split(jax.random.fold_in(seeds[2], 1), TOKENS // TOK_DEV)
    expert_ids_turns = jax.random.permutation(jax.random.fold_in(seeds[2], 3), TOKENS // TOK_DEV)
    expert_ids = jax.vmap(lambda own, number: deal_out(jax.random.fold_in(seeds[2], 2), own, number, TOK_DEV, EXPERTS, TOPK, CAP, 1))(expert_ids_keys, expert_ids_turns).reshape((TOKENS, TOPK))
    gate_weight = centred(seeds[3], (EXPERTS, D, FF), D ** -0.5, 0.125, ((0, 32),))
    up_weight = centred(seeds[4], (EXPERTS, D, FF), D ** -0.5, 0.125, ((0, 32),))
    down_weight = centred(seeds[5], (EXPERTS, FF, D), FF ** -0.5, 0.21875, ((0, 32),))
    return {"tokens": tokens, "router_weight": router_weight, "expert_ids": expert_ids, "gate_weight": gate_weight, "up_weight": up_weight, "down_weight": down_weight}


def slots_of(flat_ids):
    onehot = (flat_ids[:, :, None] == jnp.arange(EXPERTS, dtype=jnp.int32)[None, None, :]).astype(jnp.int32)
    counted = jnp.cumsum(onehot, axis=1)
    return jnp.sum(counted * onehot, axis=2) - 1


def reference(tokens, router_weight, expert_ids, gate_weight, up_weight, down_weight):
    blocks = TOKENS // TOK_DEV
    logits = jnp.dot(tokens, router_weight, preferred_element_type=jnp.float32)
    chosen = jnp.take_along_axis(logits, expert_ids, axis=1)
    weights = jnp.exp(chosen)
    gates = weights / jnp.sum(weights, axis=1, keepdims=True)
    flat_ids = expert_ids.reshape(blocks, TOK_DEV * TOPK)
    slot = slots_of(flat_ids)
    block_num = jnp.arange(blocks, dtype=jnp.int32)[:, None]
    pair_num = jnp.arange(TOK_DEV * TOPK, dtype=jnp.int32)[None, :]
    token_num = (block_num * TOK_DEV + pair_num // TOPK).astype(jnp.int32)
    position = (block_num * CAP + slot).astype(jnp.int32)
    table = jnp.zeros((EXPERTS, blocks * CAP), jnp.int32)
    table = table.at[flat_ids.reshape(-1), position.reshape(-1)].set(token_num.reshape(-1))

    def one_expert(args):
        rows_idx, w_gate, w_up, w_down = args
        rows = tokens[rows_idx]
        gate = jnp.dot(rows, w_gate, preferred_element_type=jnp.float32)
        upper = jnp.dot(rows, w_up, preferred_element_type=jnp.float32)
        hidden = (jax.nn.silu(gate) * upper).astype(jnp.bfloat16)
        return jnp.dot(hidden, w_down, preferred_element_type=jnp.float32).astype(jnp.bfloat16)

    outputs = lax.map(one_expert, (table, gate_weight, up_weight, down_weight))
    pair_expert = expert_ids
    pair_pos = position.reshape(TOKENS, TOPK)
    total = jnp.zeros((TOKENS, D), jnp.float32)
    for k in range(TOPK):
        picked = outputs[pair_expert[:, k], pair_pos[:, k]].astype(jnp.float32)
        total = total + gates[:, k:k + 1] * picked
    return total.astype(jnp.bfloat16)
```

```python
import jax
import jax.numpy as jnp
from jax import lax
from jax.sharding import Mesh
from jax.sharding import PartitionSpec as P

CHUNKS = 2


def capacity_of(tok_rows, topk, experts):
    return 5 * tok_rows * topk // (4 * experts)


def slot_matrix(ids, expert, capacity):
    has = jnp.any(ids == expert, axis=2)
    rows = ids.shape[1]
    before = jnp.arange(rows)[:, None] < jnp.arange(rows)[None, :]
    slot = jnp.dot(
        has.astype(jnp.bfloat16), before.astype(jnp.bfloat16), preferred_element_type=jnp.float32
    ).astype(jnp.int32)
    pick = (slot[:, None, :] == jnp.arange(capacity, dtype=jnp.int32)[None, :, None]) & has[:, None, :]
    return pick


def per_device(tokens, router_weight, expert_ids, gate_weight, up_weight, down_weight):
    tok_rows, width = tokens.shape
    topk = expert_ids.shape[1]
    chips = lax.axis_size("expert") * lax.axis_size("chip")
    cores = lax.axis_size("core")
    experts = chips * cores
    capacity = capacity_of(tok_rows, topk, experts)
    me = (lax.axis_index("expert") * lax.axis_size("chip") + lax.axis_index("chip")) * cores + lax.axis_index("core")
    other = me + 1 - 2 * lax.axis_index("core")
    swap = [(i, cores - 1 - i) for i in range(cores)]

    ids = lax.all_gather(expert_ids, ("expert", "chip"), axis=0, tiled=False)
    router = lax.all_gather(router_weight, ("chip", "core"), axis=0, tiled=True)
    logits = jnp.dot(tokens, router, preferred_element_type=jnp.float32)
    onehot = expert_ids[:, :, None] == jnp.arange(experts, dtype=jnp.int32)[None, None, :]
    chosen = jnp.sum(jnp.where(onehot, logits[:, None, :], 0.0), axis=2)
    weights = jnp.exp(chosen)
    gates = weights / jnp.sum(weights, axis=1, keepdims=True)
    all_gates = lax.all_gather(gates, ("expert", "chip"), axis=0, tiled=False)

    pick_me = slot_matrix(ids, me, capacity)
    pick_other = slot_matrix(ids, other, capacity)

    def gate_rows(expert):
        return jnp.sum(jnp.where(ids == expert, all_gates, 0.0), axis=2)

    picks = jnp.concatenate([pick_me, pick_other], axis=1).astype(jnp.bfloat16)

    step = width // CHUNKS
    gate = up = None
    for c in range(CHUNKS):
        cols = slice(c * step, (c + 1) * step)
        part = lax.all_gather(tokens[:, cols], ("expert", "chip"), axis=0, tiled=False)
        rows = jnp.einsum("bst,btd->bsd", picks, part, preferred_element_type=jnp.float32).astype(jnp.bfloat16)
        mine = rows[:, :capacity]
        theirs = lax.ppermute(rows[:, capacity:], "core", swap)
        x = jnp.concatenate([mine, theirs], axis=0).reshape(2 * chips * capacity, step)
        g = jnp.dot(x, gate_weight[0, cols], preferred_element_type=jnp.float32)
        u = jnp.dot(x, up_weight[0, cols], preferred_element_type=jnp.float32)
        gate = g if gate is None else gate + g
        up = u if up is None else up + u
    hidden = (jax.nn.silu(gate) * up).astype(jnp.bfloat16)

    scale_me = gate_rows(me)[:, None, :] * pick_me
    scale_other = gate_rows(other)[:, None, :] * pick_other
    mix = jnp.concatenate([scale_me, scale_other], axis=1).astype(jnp.bfloat16)
    outs = []
    for c in range(CHUNKS):
        cols = slice(c * step, (c + 1) * step)
        y = jnp.dot(hidden, down_weight[0][:, cols], preferred_element_type=jnp.float32).astype(jnp.bfloat16)
        y = y.reshape(2, chips, capacity, step)
        back = lax.ppermute(y[1], "core", swap)
        both = jnp.concatenate([y[0], back], axis=1)
        partial = jnp.einsum("bst,bsd->btd", mix, both, preferred_element_type=jnp.float32).astype(jnp.bfloat16)
        outs.append(
            lax.psum_scatter(partial, ("expert", "chip"), scatter_dimension=0, tiled=False)
        )
    return jnp.concatenate(outs, axis=1)


def solution(mesh):
    n_expert, n_zero = mesh.devices.shape
    inner = Mesh(mesh.devices.reshape(n_expert, n_zero // 2, 2), ("expert", "chip", "core"))
    everything = ("expert", "chip", "core")
    in_specs = (
        P(everything, None),
        P(("chip", "core"), None),
        P(everything, None),
        P(everything, None, None),
        P(everything, None, None),
        P(everything, None, None),
    )
    return jax.shard_map(
        per_device, mesh=inner, in_specs=in_specs, out_specs=P(everything, None), check_vma=False
    )
```

```python
import jax
import jax.numpy as jnp
from jax import lax
from jax.sharding import PartitionSpec as P

BF16 = jnp.bfloat16
F32 = jnp.float32


def expert_rows(rows, gate_weight, up_weight, down_weight):
    gate = jnp.dot(rows, gate_weight, preferred_element_type=F32)
    upper = jnp.dot(rows, up_weight, preferred_element_type=F32)
    hidden = (jax.nn.silu(gate) * upper).astype(BF16)
    return jnp.dot(hidden, down_weight, preferred_element_type=F32).astype(BF16)


def per_device(tokens, router_weight, expert_ids, gate_weight, up_weight, down_weight):
    tok_rows, width = tokens.shape
    topk = expert_ids.shape[1]
    layers = lax.axis_size("expert")
    near = lax.axis_size("zero")
    experts = layers * near
    capacity = 5 * tok_rows * topk // (4 * experts)
    layer = lax.axis_index("expert")
    mine = layer * near + jnp.arange(near, dtype=jnp.int32)
    before = (jnp.arange(tok_rows)[None, :] < jnp.arange(tok_rows)[:, None]).astype(BF16)

    def along(array, d):
        return lax.ppermute(array, "expert", [(i, (i + d) % layers) for i in range(layers)])

    order = list(range(1, layers))
    order.sort(key=lambda d: min(d, layers - d))
    blocks, ids = {0: tokens}, {0: expert_ids}
    for d in order:
        ids[d] = along(expert_ids, d)
    for d in order:
        blocks[d] = along(tokens, d)

    def pick_of(block_ids):
        has = jnp.any(block_ids[:, :, None] == mine[None, None, :], axis=1)
        slot = jnp.dot(before, has.astype(BF16), preferred_element_type=F32)
        slot = jnp.where(has, slot, -1.0).T
        return slot[:, None, :] == jnp.arange(capacity, dtype=F32)[None, :, None]

    def exchange(slabs):
        return lax.all_to_all(slabs, "zero", split_axis=0, concat_axis=0, tiled=True)

    extra = -(-router_weight.size // width)
    extra_pad = -(-extra // 8) * 8
    ride = jnp.pad(router_weight.reshape(extra, width), ((0, extra_pad - extra), (0, 0)))

    picks, received = {}, {}
    for d in [0] + order:
        picks[d] = pick_of(ids[d])
        slabs = jnp.einsum("zst,td->zsd", picks[d].astype(BF16), blocks[d], preferred_element_type=F32).astype(BF16)
        if d == 0:
            slabs = jnp.concatenate([slabs, jnp.broadcast_to(ride[None], (near, extra_pad, width))], axis=1)
        received[d] = exchange(slabs)
    router = received[0][:, capacity : capacity + extra].reshape(width, experts)
    received[0] = received[0][:, :capacity]

    total = None
    for d in order + [0]:
        logits = jnp.dot(blocks[d], router, preferred_element_type=F32)
        chosen = jnp.any(ids[d][:, :, None] == jnp.arange(experts, dtype=jnp.int32)[None, None, :], axis=1)
        weights = jnp.where(chosen, jnp.exp(jnp.where(chosen, logits, 0.0)), 0.0)
        gates = weights / jnp.sum(weights, axis=1, keepdims=True)
        gates = lax.dynamic_slice_in_dim(gates, layer * near, near, axis=1).T
        mix = (picks[d] * gates[:, None, :]).astype(BF16)

        rows = received[d].reshape(near * capacity, width)
        result = expert_rows(rows, gate_weight[0], up_weight[0], down_weight[0])
        back = exchange(result.reshape(near, capacity, width))
        partial = jnp.einsum("zst,zsd->td", mix, back, preferred_element_type=F32)
        if d:
            partial = along(partial.astype(BF16), (layers - d) % layers).astype(F32)
        total = partial if total is None else total + partial
    return total.astype(BF16)


def solution(mesh):
    everything = ("expert", "zero")
    in_specs = (
        P(everything, None),
        P("zero", None),
        P(everything, None),
        P(everything, None, None),
        P(everything, None, None),
        P(everything, None, None),
    )
    return jax.shard_map(
        per_device, mesh=mesh, in_specs=in_specs, out_specs=P(everything, None), check_vma=False
    )
```

```python
import functools

import jax
import jax.numpy as jnp
from jax import lax
from jax.experimental import pallas as pl
from jax.experimental.pallas import tpu as pltpu
from jax.sharding import PartitionSpec as P

BF16 = jnp.bfloat16
F32 = jnp.float32
VMEM_LIMIT = 40 * 1024 * 1024
STEPS = 4


def small_cost():
    return pl.CostEstimate(flops=1000, bytes_accessed=1000, transcendentals=0)


def params():
    return pltpu.CompilerParams(vmem_limit_bytes=VMEM_LIMIT)


def round_up(n, m):
    return -(-n // m) * m


def near_expert(near, offset):
    return lax.axis_index("expert") * near + lax.bitwise_xor(lax.axis_index("zero"), offset)


def slot_rows(ids_t, near, cap, cap_pad):
    toks = ids_t.shape[1]
    has = jnp.concatenate(
        [
            jnp.max((ids_t == near_expert(near, o)).astype(F32), axis=0, keepdims=True)
            for o in range(near)
        ],
        axis=0,
    )
    earlier = (
        lax.broadcasted_iota(jnp.int32, (toks, toks), 0)
        < lax.broadcasted_iota(jnp.int32, (toks, toks), 1)
    ).astype(F32).astype(BF16)
    slot = jnp.dot(has.astype(BF16), earlier, preferred_element_type=F32)
    slot = jnp.where(has > 0, slot, -1.0)
    row = lax.broadcasted_iota(jnp.int32, (cap_pad, toks), 0).astype(F32)
    return [jnp.where(row == slot[o : o + 1, :], 1.0, 0.0) for o in range(near)]


def pick_kernel(near, cap, cap_pad, ride, tokens_ref, ids_ref, *refs):
    if ride:
        router_ref, outs = refs[0], refs[1:]
    else:
        outs = refs
    picks = jnp.concatenate(slot_rows(ids_ref[...], near, cap, cap_pad), axis=0).astype(BF16)
    width = tokens_ref.shape[1]
    part = width // STEPS
    for c in range(STEPS):
        cols = slice(c * part, (c + 1) * part)
        rows = jnp.dot(picks, tokens_ref[:, cols], preferred_element_type=F32)
        for o in range(near):
            outs[o][0:cap_pad, cols] = rows[o * cap_pad : (o + 1) * cap_pad].astype(BF16)
    if ride:
        experts, depth = router_ref.shape
        per_row = width // depth
        for g in range(experts // 8):
            r, q = g // per_row, g % per_row
            piece = router_ref[8 * g : 8 * g + 8, :]
            for o in range(near):
                outs[o][cap_pad + 8 * r : cap_pad + 8 * r + 8, q * depth : (q + 1) * depth] = piece


def pick_rows(tokens, ids_t, near, cap, cap_pad, router_t=None):
    width = tokens.shape[1]
    extra = 0
    args = [tokens, ids_t]
    if router_t is not None:
        extra = round_up(router_t.shape[0] // 8 * router_t.shape[1], width) // width * 8
        args.append(router_t)
    vmem = pl.BlockSpec(memory_space=pltpu.VMEM)
    return pl.pallas_call(
        functools.partial(pick_kernel, near, cap, cap_pad, router_t is not None),
        out_shape=[jax.ShapeDtypeStruct((cap_pad + extra, width), BF16)] * near,
        in_specs=[vmem] * len(args),
        out_specs=[vmem] * near,
        compiler_params=params(),
        cost_estimate=small_cost(),
    )(*args)


def expert_kernel(near, rows_each, *refs):
    xs = refs[:near]
    gate_ref, up_ref, down_ref = refs[near : near + 3]
    outs = refs[near + 3 : 2 * near + 3]
    gate_sum, up_sum, hidden = refs[2 * near + 3 :]
    step = pl.program_id(0)

    @pl.when(step < STEPS)
    def _():
        x = jnp.concatenate([r[0:rows_each, :].astype(F32) for r in xs], axis=0).astype(BF16)
        gate = jnp.dot(x, gate_ref[...], preferred_element_type=F32)
        upper = jnp.dot(x, up_ref[...], preferred_element_type=F32)

        @pl.when(step == 0)
        def _():
            gate_sum[...] = gate
            up_sum[...] = upper

        @pl.when((step > 0) & (step < STEPS - 1))
        def _():
            gate_sum[...] += gate
            up_sum[...] += upper

        @pl.when(step == STEPS - 1)
        def _():
            v = gate_sum[...] + gate
            hidden[...] = (v / (1.0 + jnp.exp(-v)) * (up_sum[...] + upper)).astype(BF16)

    @pl.when(step >= STEPS)
    def _():
        y = jnp.dot(hidden[...], down_ref[...], preferred_element_type=F32)
        for o in range(near):
            outs[o][...] = y[o * rows_each : (o + 1) * rows_each].astype(BF16)


def run_expert(xs, gate_weight, up_weight, down_weight, rows_each):
    near = len(xs)
    width, ff = gate_weight.shape
    part = width // STEPS
    first = lambda i: jnp.minimum(i, STEPS - 1)
    second = lambda i: jnp.maximum(i - STEPS, 0)
    return pl.pallas_call(
        functools.partial(expert_kernel, near, rows_each),
        grid=(2 * STEPS,),
        out_shape=[jax.ShapeDtypeStruct((rows_each, width), BF16)] * near,
        in_specs=[pl.BlockSpec((x.shape[0], part), lambda i: (0, first(i))) for x in xs]
        + [pl.BlockSpec((part, ff), lambda i: (first(i), 0))] * 2
        + [pl.BlockSpec((ff, part), lambda i: (0, second(i)))],
        out_specs=[pl.BlockSpec((rows_each, part), lambda i: (0, second(i)))] * near,
        scratch_shapes=[
            pltpu.VMEM((near * rows_each, ff), F32),
            pltpu.VMEM((near * rows_each, ff), F32),
            pltpu.VMEM((near * rows_each, ff), BF16),
        ],
        compiler_params=params(),
        cost_estimate=small_cost(),
    )(*xs, gate_weight, up_weight, down_weight)


def mix_kernel(near, cap, cap_pad, depth, experts, tokens_ref, ids_ref, *refs):
    riders, backs, out = refs[:near], refs[near : 2 * near], refs[2 * near]
    ids_t = ids_ref[...]
    topk, toks = ids_t.shape
    width = tokens_ref.shape[1]
    per_row = width // depth
    logits = None
    for o in range(near):
        start = pl.multiple_of(lax.bitwise_xor(lax.axis_index("zero"), o) * depth, depth)
        pieces = []
        for g in range(experts // 8):
            r, q = g // per_row, g % per_row
            pieces.append(
                riders[o][cap_pad + 8 * r : cap_pad + 8 * r + 8, q * depth : (q + 1) * depth].astype(F32)
            )
        router_t = jnp.concatenate(pieces, axis=0).astype(BF16)
        term = lax.dot_general(
            router_t, tokens_ref[:, pl.ds(start, depth)], (((1,), (1,)), ((), ())), preferred_element_type=F32
        )
        logits = term if logits is None else logits + term
    number = lax.broadcasted_iota(jnp.int32, (experts, toks), 0)
    chosen = number == ids_t[0:1, :]
    for k in range(1, topk):
        chosen = chosen | (number == ids_t[k : k + 1, :])
    weights = jnp.where(chosen, jnp.exp(jnp.where(chosen, logits, 0.0)), 0.0)
    gates = weights / jnp.sum(weights, axis=0, keepdims=True)
    picks = slot_rows(ids_t, near, cap, cap_pad)
    mix = []
    for o in range(near):
        gate = jnp.sum(jnp.where(number == near_expert(near, o), gates, 0.0), axis=0, keepdims=True)
        mix.append(picks[o] * gate)
    mix = jnp.concatenate(mix, axis=0).astype(BF16)
    part = width // STEPS
    for c in range(STEPS):
        cols = slice(c * part, (c + 1) * part)
        y = jnp.concatenate([b[:, cols].astype(F32) for b in backs], axis=0).astype(BF16)
        out[:, cols] = lax.dot_general(
            mix, y, (((0,), (0,)), ((), ())), preferred_element_type=F32
        ).astype(BF16)


def mix_rows(tokens, ids_t, riders, backs, cap, cap_pad, depth, experts):
    near = len(backs)
    vmem = pl.BlockSpec(memory_space=pltpu.VMEM)
    return pl.pallas_call(
        functools.partial(mix_kernel, near, cap, cap_pad, depth, experts),
        out_shape=jax.ShapeDtypeStruct(tokens.shape, BF16),
        in_specs=[vmem] * (2 + 2 * near),
        out_specs=vmem,
        compiler_params=params(),
        cost_estimate=small_cost(),
    )(tokens, ids_t, *riders, *backs)


def per_device(tokens, router_weight, expert_ids, gate_weight, up_weight, down_weight):
    tok_rows, width = tokens.shape
    topk = expert_ids.shape[1]
    layers = lax.axis_size("expert")
    near = lax.axis_size("zero")
    experts = layers * near
    cap = 5 * tok_rows * topk // (4 * experts)
    cap_pad = round_up(cap, 8)
    depth = router_weight.shape[0]

    def along(array, d):
        return lax.ppermute(array, "expert", [(i, (i + d) % layers) for i in range(layers)])

    def across(array, o):
        return lax.ppermute(array, "zero", [(i, i ^ o) for i in range(near)]) if o else array

    order = sorted(range(1, layers), key=lambda d: -min(d, layers - d))
    blocks, ids = {0: tokens}, {0: expert_ids.T}
    for d in order:
        ids[d] = along(ids[0], d)
    source = tokens
    for d in order:
        blocks[d] = along(source, d)
        source, _ = lax.optimization_barrier((tokens, blocks[d]))

    received, results, partial = {}, {}, {}
    for d in [0] + order:
        router_t = None if d else router_weight.T
        slabs = pick_rows(blocks[d], ids[d], near, cap, cap_pad, router_t)
        received[d] = [across(s, o) for o, s in enumerate(slabs)]
    for d in [0] + order:
        results[d] = run_expert(received[d], gate_weight[0], up_weight[0], down_weight[0], cap_pad)
    for d in order + [0]:
        backs = [across(r, o) for o, r in enumerate(results[d])]
        mixed = mix_rows(blocks[d], ids[d], received[0], backs, cap, cap_pad, depth, experts)
        partial[d] = along(mixed, layers - d) if d else mixed
    total = partial[0].astype(F32)
    for d in order:
        total = total + partial[d].astype(F32)
    return total.astype(BF16)


def solution(mesh):
    everything = ("expert", "zero")
    in_specs = (
        P(everything, None),
        P("zero", None),
        P(everything, None),
        P(everything, None, None),
        P(everything, None, None),
        P(everything, None, None),
    )
    return jax.shard_map(
        per_device, mesh=mesh, in_specs=in_specs, out_specs=P(everything, None), check_vma=False
    )
```

```python
import functools

import jax
import jax.numpy as jnp
from jax import lax
from jax.experimental import pallas as pl
from jax.experimental.pallas import tpu as pltpu
from jax.sharding import PartitionSpec as P

BF16 = jnp.bfloat16
F32 = jnp.float32
VMEM_LIMIT = 32 * 1024 * 1024
PARTS = 4
CORES = 2
VMEM = pl.BlockSpec(memory_space=pltpu.VMEM)


def call(body, out_shape, n_in, scratch=()):
    many = isinstance(out_shape, list)
    return pl.pallas_call(
        body,
        out_shape=out_shape,
        in_specs=[VMEM] * n_in,
        out_specs=[VMEM] * len(out_shape) if many else VMEM,
        scratch_shapes=list(scratch),
        compiler_params=pltpu.CompilerParams(vmem_limit_bytes=VMEM_LIMIT),
        cost_estimate=pl.CostEstimate(flops=1000, bytes_accessed=1000, transcendentals=0),
    )


def round_up(n, m):
    return -(-n // m) * m


class Sizes:
    def __init__(self, tokens, router_t, ids_t, near, layers):
        self.toks, self.width = tokens.shape
        self.experts, self.depth = router_t.shape
        self.topk = ids_t.shape[0]
        self.near, self.layers = near, layers
        self.chips = near // CORES
        self.cap = round_up(5 * self.toks * self.topk // (4 * self.experts), 8)
        self.tiles = self.width // self.depth
        self.extra = -(-(1 + self.experts // 8) // self.tiles) * 8

    def tile(self, g):
        r, q = g // self.tiles * 8, g % self.tiles * self.depth
        return slice(r, r + 8), slice(q, q + self.depth)


def pad_kernel(z, tokens_ref, ids_ref, router_ref, out):
    out[0 : z.toks, :] = tokens_ref[...]
    blank = jnp.zeros((z.extra, z.width), BF16)
    out[z.toks : z.toks + z.extra, :] = blank
    out[z.toks : z.toks + 8, 0 : z.toks] = ids_ref[...].astype(F32).astype(BF16)
    for g in range(z.experts // 8):
        rows, cols = z.tile(g + 1)
        out[z.toks + rows.start : z.toks + rows.stop, cols] = router_ref[8 * g : 8 * g + 8, :]


def served_expert(z, q):
    return lax.axis_index("expert") * z.near + lax.bitwise_xor(lax.axis_index("zero"), q * CORES)


def ids_of(z, block_ref):
    return block_ref[z.toks : z.toks + 8, 0 : z.toks].astype(F32).astype(jnp.int32)


def slot_marks(z, ids_t):
    has = jnp.concatenate(
        [
            jnp.max((ids_t == served_expert(z, q)).astype(F32), axis=0, keepdims=True)
            for q in range(z.chips)
        ]
        * 2,
        axis=0,
    )
    earlier = (
        lax.broadcasted_iota(jnp.int32, (z.toks, z.toks), 0)
        < lax.broadcasted_iota(jnp.int32, (z.toks, z.toks), 1)
    ).astype(F32).astype(BF16)
    slot = jnp.dot(has.astype(BF16), earlier, preferred_element_type=F32)
    slot = jnp.where(has > 0, slot, -1.0)
    row = lax.broadcasted_iota(jnp.int32, (z.cap, z.toks), 0).astype(F32)
    return [jnp.where(row == slot[q : q + 1, :], 1.0, 0.0) for q in range(z.chips)]


def pick_kernel(z, n, ride, *refs):
    blocks, outs = refs[:n], refs[n:]
    marks = [jnp.concatenate(slot_marks(z, ids_of(z, b)), axis=0).astype(BF16) for b in blocks]
    part = z.width // PARTS
    for c in range(PARTS):
        cols = slice(c * part, (c + 1) * part)
        rows = [jnp.dot(m, b[0 : z.toks, cols], preferred_element_type=F32) for m, b in zip(marks, blocks)]
        for q in range(z.chips):
            mine = [r[q * z.cap : (q + 1) * z.cap] for r in rows]
            outs[q][0 : n * z.cap, cols] = jnp.concatenate(mine, axis=0).astype(BF16)
    if ride:
        for q in range(z.chips):
            for r in range(CORES):
                start = n * z.cap + r * z.extra
                outs[q][start : start + z.extra, :] = blocks[r][z.toks : z.toks + z.extra, :]


def expert_kernel(z, rows, *refs):
    slabs, gate_ref, up_ref, down_ref = refs[: z.chips], *refs[z.chips : z.chips + 3]
    outs, (x, hidden) = refs[z.chips + 3 : 2 * z.chips + 3], refs[2 * z.chips + 3 :]
    for q in range(z.chips):
        x[q * rows : (q + 1) * rows, :] = slabs[q][0:rows, :]
    ff = gate_ref.shape[1]
    tile = 256
    for f in range(0, ff, tile):
        gate = jnp.dot(x[...], gate_ref[:, f : f + tile], preferred_element_type=F32)
        upper = jnp.dot(x[...], up_ref[:, f : f + tile], preferred_element_type=F32)
        hidden[:, f : f + tile] = (gate / (1.0 + jnp.exp(-gate)) * upper).astype(BF16)
    for c in range(0, z.width, tile):
        y = jnp.dot(hidden[...], down_ref[:, c : c + tile], preferred_element_type=F32)
        for q in range(z.chips):
            outs[q][:, c : c + tile] = y[q * rows : (q + 1) * rows].astype(BF16)


def mix_kernel(z, n, *refs):
    blocks, refs = refs[:n], refs[n:]
    riders, backs, outs = refs[: z.chips], refs[z.chips : 2 * z.chips], refs[2 * z.chips :]
    number = lax.broadcasted_iota(jnp.int32, (z.experts, z.toks), 0)
    routers = []
    for q in range(z.chips):
        for r in range(CORES):
            base = CORES * z.cap + r * z.extra
            pieces = []
            for g in range(z.experts // 8):
                rows, cols = z.tile(g + 1)
                pieces.append(riders[q][base + rows.start : base + rows.stop, cols].astype(F32))
            routers.append(jnp.concatenate(pieces, axis=0).astype(BF16))
    for b, block in enumerate(blocks):
        out, base = outs[b % CORES], b // CORES * z.toks
        ids_t = ids_of(z, block)
        logits = None
        for o in range(z.near):
            start = pl.multiple_of(lax.bitwise_xor(lax.axis_index("zero"), o) * z.depth, z.depth)
            term = lax.dot_general(
                routers[o],
                block[0 : z.toks, pl.ds(start, z.depth)],
                (((1,), (1,)), ((), ())),
                preferred_element_type=F32,
            )
            logits = term if logits is None else logits + term
        chosen = number == ids_t[0:1, :]
        for k in range(1, z.topk):
            chosen = chosen | (number == ids_t[k : k + 1, :])
        weights = jnp.where(chosen, jnp.exp(jnp.where(chosen, logits, 0.0)), 0.0)
        gates = weights / jnp.sum(weights, axis=0, keepdims=True)
        marks = slot_marks(z, ids_t)
        mix = []
        for q in range(z.chips):
            gate = jnp.sum(jnp.where(number == served_expert(z, q), gates, 0.0), axis=0, keepdims=True)
            mix.append(marks[q] * gate)
        mix = jnp.concatenate(mix, axis=0).astype(BF16)
        part = z.width // PARTS
        for c in range(PARTS):
            cols = slice(c * part, (c + 1) * part)
            own = slice(b * z.cap, (b + 1) * z.cap)
            y = jnp.concatenate([s[:, cols].astype(F32)[own] for s in backs], axis=0).astype(BF16)
            out[base : base + z.toks, cols] = lax.dot_general(
                mix, y, (((0,), (0,)), ((), ())), preferred_element_type=F32
            ).astype(BF16)


def per_device(tokens, router_weight, expert_ids, gate_weight, up_weight, down_weight):
    layers, near = lax.axis_size("expert"), lax.axis_size("zero")
    z = Sizes(tokens, router_weight.T, expert_ids.T, near, layers)

    def along(array, d):
        return lax.ppermute(array, "expert", [(i, (i + d) % layers) for i in range(layers)])

    def across(array, o):
        return lax.ppermute(array, "zero", [(i, i ^ o) for i in range(near)]) if o else array

    def after(arrays, *others):
        return list(lax.optimization_barrier((*arrays, *others))[: len(arrays)])

    def shape(rows):
        return jax.ShapeDtypeStruct((rows, z.width), BF16)

    def pick(blocks, ride):
        n = len(blocks)
        rows = n * z.cap + (CORES * z.extra if ride else 0)
        return call(functools.partial(pick_kernel, z, n, ride), [shape(rows)] * z.chips, n)(*blocks)

    def slabs_across(slabs):
        return [across(s, CORES * q) for q, s in enumerate(slabs)]

    def expert(slabs, n):
        rows = n * z.cap
        return call(
            functools.partial(expert_kernel, z, rows),
            [shape(rows)] * z.chips,
            z.chips + 3,
            [
                pltpu.VMEM((z.chips * rows, z.width), BF16),
                pltpu.VMEM((z.chips * rows, gate_weight.shape[2]), BF16),
            ],
        )(*slabs, gate_weight[0], up_weight[0], down_weight[0])

    def mix(blocks, backs):
        n = len(blocks)
        mine, other = call(
            functools.partial(mix_kernel, z, n), [shape(n // 2 * z.toks)] * 2, n + 2 * z.chips
        )(*blocks, *riders, *backs)
        other = across(other, 1)
        return [
            mine[i * z.toks : (i + 1) * z.toks].astype(F32) + other[i * z.toks : (i + 1) * z.toks].astype(F32)
            for i in range(n // 2)
        ]

    half = layers // 2
    groups = [sorted({d, layers - d}) for d in range(1, half + 1)]

    own = call(functools.partial(pad_kernel, z), shape(z.toks + z.extra), 3)(
        tokens, expert_ids.T, router_weight.T
    )
    pairs, slots, results = {}, {}, {}
    coming = [along(own, d) for d in groups[0]]
    pairs[0] = [own, across(own, 1)]
    slots[0] = slabs_across(pick(pairs[0], True))
    riders = slots[0]
    for g in range(1, len(groups) + 1):
        blocks = coming
        if g < len(groups):
            source = after([own], *blocks, *slots[g - 1])[0]
            coming = [along(source, d) for d in groups[g]]
        pairs[g] = [b for block in blocks for b in (block, across(block, 1))]
        slabs = after(pick(pairs[g], False), *slots[g - 1])
        slots[g] = slabs_across(slabs)
        results[g - 1] = expert(after(slots[g - 1], slabs[1]), len(pairs[g - 1]))
    results[g] = expert(slots[g], len(pairs[g]))
    turns = list(range(1, len(groups) + 1)) + [0]
    backs, leaving, home = [], [], {}
    for g, later in zip(turns, turns[1:] + turns[:1]):
        rows = after(results[g], *backs) if backs else results[g]
        backs = slabs_across(rows)
        if g:
            ready = after(backs, results[later][1], *leaving)
            sums = mix(pairs[g], ready)
            leaving = [part.astype(BF16) for part in sums]
            for d, part in zip(groups[g - 1], leaving):
                home[d] = along(part, layers - d)
        else:
            early = [home[d] for group in groups[:-1] for d in group]
            total = mix(pairs[0], after(backs, *early))[0]
    for d in home:
        total = total + home[d].astype(F32)
    return total.astype(BF16)


def solution(mesh):
    everything = ("expert", "zero")
    in_specs = (
        P(everything, None),
        P("zero", None),
        P(everything, None),
        P(everything, None, None),
        P(everything, None, None),
        P(everything, None, None),
    )
    return jax.shard_map(
        per_device, mesh=mesh, in_specs=in_specs, out_specs=P(everything, None), check_vma=False
    )
```

```python
import functools

import jax
import jax.numpy as jnp
from jax import lax
from jax.experimental import pallas as pl
from jax.experimental.pallas import tpu as pltpu
from jax.sharding import PartitionSpec as P

BF16 = jnp.bfloat16
F32 = jnp.float32
VMEM_LIMIT = 32 * 1024 * 1024
PARTS = 4
CORES = 2
VMEM = pl.BlockSpec(memory_space=pltpu.VMEM)


def call(body, out_shape, n_in, scratch=()):
    many = isinstance(out_shape, list)
    return pl.pallas_call(
        body,
        out_shape=out_shape,
        in_specs=[VMEM] * n_in,
        out_specs=[VMEM] * len(out_shape) if many else VMEM,
        scratch_shapes=list(scratch),
        compiler_params=pltpu.CompilerParams(vmem_limit_bytes=VMEM_LIMIT),
        cost_estimate=pl.CostEstimate(flops=1000, bytes_accessed=1000, transcendentals=0),
    )


def round_up(n, m):
    return -(-n // m) * m


class Sizes:
    def __init__(self, tokens, router_t, ids_t, near, layers):
        self.toks, self.width = tokens.shape
        self.experts, self.depth = router_t.shape
        self.topk = ids_t.shape[0]
        self.near, self.layers = near, layers
        self.chips = near // CORES
        self.cap = round_up(5 * self.toks * self.topk // (4 * self.experts), 8)
        self.tiles = self.width // self.depth
        self.extra = -(-(1 + self.experts // 8) // self.tiles) * 8

    def tile(self, g):
        r, q = g // self.tiles * 8, g % self.tiles * self.depth
        return slice(r, r + 8), slice(q, q + self.depth)


def pad_kernel(z, tokens_ref, ids_ref, router_ref, out):
    out[0 : z.toks, :] = tokens_ref[...]
    blank = jnp.zeros((z.extra, z.width), BF16)
    out[z.toks : z.toks + z.extra, :] = blank
    out[z.toks : z.toks + 8, 0 : z.toks] = ids_ref[...].astype(F32).astype(BF16)
    for g in range(z.experts // 8):
        rows, cols = z.tile(g + 1)
        out[z.toks + rows.start : z.toks + rows.stop, cols] = router_ref[8 * g : 8 * g + 8, :]


def served_expert(z, q):
    return lax.axis_index("expert") * z.near + lax.bitwise_xor(lax.axis_index("zero"), q * CORES)


def ids_of(z, block_ref):
    return block_ref[z.toks : z.toks + 8, 0 : z.toks].astype(F32).astype(jnp.int32)


def slot_marks(z, ids_t):
    has = jnp.concatenate(
        [
            jnp.max((ids_t == served_expert(z, q)).astype(F32), axis=0, keepdims=True)
            for q in range(z.chips)
        ]
        * 2,
        axis=0,
    )
    earlier = (
        lax.broadcasted_iota(jnp.int32, (z.toks, z.toks), 0)
        < lax.broadcasted_iota(jnp.int32, (z.toks, z.toks), 1)
    ).astype(F32).astype(BF16)
    slot = jnp.dot(has.astype(BF16), earlier, preferred_element_type=F32)
    slot = jnp.where(has > 0, slot, -1.0)
    row = lax.broadcasted_iota(jnp.int32, (z.cap, z.toks), 0).astype(F32)
    return [jnp.where(row == slot[q : q + 1, :], 1.0, 0.0) for q in range(z.chips)]


def pick_kernel(z, n, ride, *refs):
    blocks, outs = refs[:n], refs[n:]
    marks = [jnp.concatenate(slot_marks(z, ids_of(z, b)), axis=0).astype(BF16) for b in blocks]
    part = z.width // PARTS
    for c in range(PARTS):
        cols = slice(c * part, (c + 1) * part)
        rows = [jnp.dot(m, b[0 : z.toks, cols], preferred_element_type=F32) for m, b in zip(marks, blocks)]
        for q in range(z.chips):
            mine = [r[q * z.cap : (q + 1) * z.cap] for r in rows]
            outs[q][0 : n * z.cap, cols] = jnp.concatenate(mine, axis=0).astype(BF16)
    if ride:
        for q in range(z.chips):
            for r in range(CORES):
                start = n * z.cap + r * z.extra
                outs[q][start : start + z.extra, :] = blocks[r][z.toks : z.toks + z.extra, :]


def expert_kernel(z, rows, *refs):
    slabs, gate_ref, up_ref, down_ref = refs[: z.chips], *refs[z.chips : z.chips + 3]
    outs, (x, hidden) = refs[z.chips + 3 : 2 * z.chips + 3], refs[2 * z.chips + 3 :]
    for q in range(z.chips):
        x[q * rows : (q + 1) * rows, :] = slabs[q][0:rows, :]
    ff = gate_ref.shape[1]
    tile = 256
    for f in range(0, ff, tile):
        gate = jnp.dot(x[...], gate_ref[:, f : f + tile], preferred_element_type=F32)
        upper = jnp.dot(x[...], up_ref[:, f : f + tile], preferred_element_type=F32)
        hidden[:, f : f + tile] = (gate / (1.0 + jnp.exp(-gate)) * upper).astype(BF16)
    for c in range(0, z.width, tile):
        y = jnp.dot(hidden[...], down_ref[:, c : c + tile], preferred_element_type=F32)
        for q in range(z.chips):
            outs[q][:, c : c + tile] = y[q * rows : (q + 1) * rows].astype(BF16)


def mix_kernel(z, n, *refs):
    blocks, refs = refs[:n], refs[n:]
    riders, backs, outs = refs[: z.chips], refs[z.chips : 2 * z.chips], refs[2 * z.chips :]
    number = lax.broadcasted_iota(jnp.int32, (z.experts, z.toks), 0)
    routers = []
    for q in range(z.chips):
        for r in range(CORES):
            base = CORES * z.cap + r * z.extra
            pieces = []
            for g in range(z.experts // 8):
                rows, cols = z.tile(g + 1)
                pieces.append(riders[q][base + rows.start : base + rows.stop, cols].astype(F32))
            routers.append(jnp.concatenate(pieces, axis=0).astype(BF16))
    for b, block in enumerate(blocks):
        out, base = outs[b % CORES], b // CORES * z.toks
        ids_t = ids_of(z, block)
        logits = None
        for o in range(z.near):
            start = pl.multiple_of(lax.bitwise_xor(lax.axis_index("zero"), o) * z.depth, z.depth)
            term = lax.dot_general(
                routers[o],
                block[0 : z.toks, pl.ds(start, z.depth)],
                (((1,), (1,)), ((), ())),
                preferred_element_type=F32,
            )
            logits = term if logits is None else logits + term
        chosen = number == ids_t[0:1, :]
        for k in range(1, z.topk):
            chosen = chosen | (number == ids_t[k : k + 1, :])
        weights = jnp.where(chosen, jnp.exp(jnp.where(chosen, logits, 0.0)), 0.0)
        gates = weights / jnp.sum(weights, axis=0, keepdims=True)
        marks = slot_marks(z, ids_t)
        mix = []
        for q in range(z.chips):
            gate = jnp.sum(jnp.where(number == served_expert(z, q), gates, 0.0), axis=0, keepdims=True)
            mix.append(marks[q] * gate)
        mix = jnp.concatenate(mix, axis=0).astype(BF16)
        part = z.width // PARTS
        for c in range(PARTS):
            cols = slice(c * part, (c + 1) * part)
            own = slice(b * z.cap, (b + 1) * z.cap)
            y = jnp.concatenate([s[:, cols].astype(F32)[own] for s in backs], axis=0).astype(BF16)
            out[base : base + z.toks, cols] = lax.dot_general(
                mix, y, (((0,), (0,)), ((), ())), preferred_element_type=F32
            ).astype(BF16)


def per_device(tokens, router_weight, expert_ids, gate_weight, up_weight, down_weight):
    layers, near = lax.axis_size("expert"), lax.axis_size("zero")
    z = Sizes(tokens, router_weight.T, expert_ids.T, near, layers)

    def along(array, d):
        return lax.ppermute(array, "expert", [(i, (i + d) % layers) for i in range(layers)])

    def across(array, o):
        return lax.ppermute(array, "zero", [(i, i ^ o) for i in range(near)]) if o else array

    def after(arrays, *others):
        return list(lax.optimization_barrier((*arrays, *others))[: len(arrays)])

    def shape(rows):
        return jax.ShapeDtypeStruct((rows, z.width), BF16)

    def pick(blocks, ride):
        n = len(blocks)
        rows = n * z.cap + (CORES * z.extra if ride else 0)
        return call(functools.partial(pick_kernel, z, n, ride), [shape(rows)] * z.chips, n)(*blocks)

    def slabs_across(slabs):
        return [across(s, CORES * q) for q, s in enumerate(slabs)]

    def expert(slabs, n):
        rows = n * z.cap
        return call(
            functools.partial(expert_kernel, z, rows),
            [shape(rows)] * z.chips,
            z.chips + 3,
            [
                pltpu.VMEM((z.chips * rows, z.width), BF16),
                pltpu.VMEM((z.chips * rows, gate_weight.shape[2]), BF16),
            ],
        )(*slabs, gate_weight[0], up_weight[0], down_weight[0])

    def mix(blocks, backs):
        n = len(blocks)
        mine, other = call(
            functools.partial(mix_kernel, z, n), [shape(n // 2 * z.toks)] * 2, n + 2 * z.chips
        )(*blocks, *riders, *backs)
        other = across(other, 1)
        return [
            mine[i * z.toks : (i + 1) * z.toks].astype(F32) + other[i * z.toks : (i + 1) * z.toks].astype(F32)
            for i in range(n // 2)
        ]

    far = layers // 2
    out_turns = list(range(layers))
    back_turns = [far] + [d for d in out_turns if d not in (0, far)] + [0]

    own = call(functools.partial(pad_kernel, z), shape(z.toks + z.extra), 3)(
        tokens, expert_ids.T, router_weight.T
    )

    blocks, pairs, slots, results = {0: own}, {}, {}, {}
    for d in out_turns:
        if d:
            gone = slots[d - 2] if d > 1 else []
            blocks[d] = along(after([blocks[d - 1]], *gone)[0], 1)
        pairs[d] = [blocks[d], across(blocks[d], 1)]
        slabs = pick(pairs[d], d == 1)
        if d:
            done = results[d - 2][:1] if d > 1 else []
            ready = [after([s], b, *done)[0] for s, b in zip(slabs, slots[d - 1])]
            results[d - 1] = expert(after(slots[d - 1], slabs[0]), 2)
        else:
            ready = slabs
        slots[d] = slabs_across(ready)
    riders = slots[1]
    results[d] = expert(after(slots[d], results[d - 1][0]), 2)

    backs, home, leaving = slots[d], {}, {}
    for i, d in enumerate(back_turns):
        first = [leaving[back_turns[i - 2]]] if i > 1 else [results[layers - 2 + i][0]]
        if d == 0:
            first = first + [home[far]]
        rows = [after([r], b, *first)[0] for r, b in zip(results[d], backs)]
        backs = slabs_across(rows)
        last = leaving[back_turns[i - 1]] if i else results[layers - 1][0]
        if d:
            part = mix(pairs[d], after(backs, last))[0]
            leaving[d] = part.astype(BF16)
            way = layers - d
            if d == far:
                home[d] = along(along(leaving[d], way // 2), way - way // 2)
            else:
                home[d] = along(leaving[d], way)
    total = mix(pairs[0], after(backs, last))[0]
    for d in out_turns[1:]:
        total = total + home[d].astype(F32)
    return total.astype(BF16)


def solution(mesh):
    everything = ("expert", "zero")
    in_specs = (
        P(everything, None),
        P("zero", None),
        P(everything, None),
        P(everything, None, None),
        P(everything, None, None),
        P(everything, None, None),
    )
    return jax.shard_map(
        per_device, mesh=mesh, in_specs=in_specs, out_specs=P(everything, None), check_vma=False
    )
```

```python
import functools

import jax
import jax.numpy as jnp
from jax import lax
from jax.experimental import pallas as pl
from jax.experimental.pallas import tpu as pltpu
from jax.sharding import PartitionSpec as P

BF16 = jnp.bfloat16
F32 = jnp.float32
VMEM_LIMIT = 32 * 1024 * 1024
PARTS = 4
CORES = 2
PHASE_FLOPS = 50_000_000_000
VMEM = pl.BlockSpec(memory_space=pltpu.VMEM)


def call(body, out_shape, n_in, scratch=(), flops=1000):
    many = isinstance(out_shape, list)
    return pl.pallas_call(
        body,
        out_shape=out_shape,
        in_specs=[VMEM] * n_in,
        out_specs=[VMEM] * len(out_shape) if many else VMEM,
        scratch_shapes=list(scratch),
        compiler_params=pltpu.CompilerParams(vmem_limit_bytes=VMEM_LIMIT),
        cost_estimate=pl.CostEstimate(flops=flops, bytes_accessed=1000, transcendentals=0),
    )


def arrived_kernel(*refs):
    total = refs[0][0:8, 0:128]
    for ref in refs[1:-1]:
        total = total + ref[0:8, 0:128]
    refs[-1][...] = total


def round_up(n, m):
    return -(-n // m) * m


class Sizes:
    def __init__(self, tokens, router_t, ids_t, near, layers):
        self.toks, self.width = tokens.shape
        self.experts, self.depth = router_t.shape
        self.topk = ids_t.shape[0]
        self.near, self.layers = near, layers
        self.chips = near // CORES
        self.cap = round_up(5 * self.toks * self.topk // (4 * self.experts), 8)
        self.tiles = self.width // self.depth
        self.extra = -(-(1 + self.experts // 8) // self.tiles) * 8

    def tile(self, g):
        r, q = g // self.tiles * 8, g % self.tiles * self.depth
        return slice(r, r + 8), slice(q, q + self.depth)


def pad_kernel(z, tokens_ref, ids_ref, router_ref, out):
    out[0 : z.toks, :] = tokens_ref[...]
    blank = jnp.zeros((z.extra, z.width), BF16)
    out[z.toks : z.toks + z.extra, :] = blank
    out[z.toks : z.toks + 8, 0 : z.toks] = ids_ref[...].astype(F32).astype(BF16)
    for g in range(z.experts // 8):
        rows, cols = z.tile(g + 1)
        out[z.toks + rows.start : z.toks + rows.stop, cols] = router_ref[8 * g : 8 * g + 8, :]


def served_expert(z, q):
    return lax.axis_index("expert") * z.near + lax.bitwise_xor(lax.axis_index("zero"), q * CORES)


def ids_of(z, block_ref):
    return block_ref[z.toks : z.toks + 8, 0 : z.toks].astype(F32).astype(jnp.int32)


def slot_marks(z, ids_t):
    has = jnp.concatenate(
        [
            jnp.max((ids_t == served_expert(z, q)).astype(F32), axis=0, keepdims=True)
            for q in range(z.chips)
        ]
        * 2,
        axis=0,
    )
    earlier = (
        lax.broadcasted_iota(jnp.int32, (z.toks, z.toks), 0)
        < lax.broadcasted_iota(jnp.int32, (z.toks, z.toks), 1)
    ).astype(F32).astype(BF16)
    slot = jnp.dot(has.astype(BF16), earlier, preferred_element_type=F32)
    slot = jnp.where(has > 0, slot, -1.0)
    row = lax.broadcasted_iota(jnp.int32, (z.cap, z.toks), 0).astype(F32)
    return [jnp.where(row == slot[q : q + 1, :], 1.0, 0.0) for q in range(z.chips)]


def pick_kernel(z, n, ride, *refs):
    blocks, outs = refs[:n], refs[n:]
    marks = [jnp.concatenate(slot_marks(z, ids_of(z, b)), axis=0).astype(BF16) for b in blocks]
    part = z.width // PARTS
    for c in range(PARTS):
        cols = slice(c * part, (c + 1) * part)
        rows = [jnp.dot(m, b[0 : z.toks, cols], preferred_element_type=F32) for m, b in zip(marks, blocks)]
        for q in range(z.chips):
            mine = [r[q * z.cap : (q + 1) * z.cap] for r in rows]
            outs[q][0 : n * z.cap, cols] = jnp.concatenate(mine, axis=0).astype(BF16)
    if ride:
        for q in range(z.chips):
            for r in range(CORES):
                start = n * z.cap + r * z.extra
                outs[q][start : start + z.extra, :] = blocks[r][z.toks : z.toks + z.extra, :]


def expert_kernel(z, rows, *refs):
    slabs, gate_ref, up_ref, down_ref = refs[: z.chips], *refs[z.chips : z.chips + 3]
    outs, (x, hidden) = refs[z.chips + 3 : 2 * z.chips + 3], refs[2 * z.chips + 3 :]
    for q in range(z.chips):
        x[q * rows : (q + 1) * rows, :] = slabs[q][0:rows, :]
    ff = gate_ref.shape[1]
    tile = 256
    for f in range(0, ff, tile):
        gate = jnp.dot(x[...], gate_ref[:, f : f + tile], preferred_element_type=F32)
        upper = jnp.dot(x[...], up_ref[:, f : f + tile], preferred_element_type=F32)
        hidden[:, f : f + tile] = (gate / (1.0 + jnp.exp(-gate)) * upper).astype(BF16)
    for c in range(0, z.width, tile):
        y = jnp.dot(hidden[...], down_ref[:, c : c + tile], preferred_element_type=F32)
        for q in range(z.chips):
            outs[q][:, c : c + tile] = y[q * rows : (q + 1) * rows].astype(BF16)


def mix_kernel(z, n, *refs):
    blocks, refs = refs[:n], refs[n:]
    riders, backs, outs = refs[: z.chips], refs[z.chips : 2 * z.chips], refs[2 * z.chips :]
    number = lax.broadcasted_iota(jnp.int32, (z.experts, z.toks), 0)
    routers = []
    for q in range(z.chips):
        for r in range(CORES):
            base = CORES * z.cap + r * z.extra
            pieces = []
            for g in range(z.experts // 8):
                rows, cols = z.tile(g + 1)
                pieces.append(riders[q][base + rows.start : base + rows.stop, cols].astype(F32))
            routers.append(jnp.concatenate(pieces, axis=0).astype(BF16))
    for b, block in enumerate(blocks):
        out, base = outs[b % CORES], b // CORES * z.toks
        ids_t = ids_of(z, block)
        logits = None
        for o in range(z.near):
            start = pl.multiple_of(lax.bitwise_xor(lax.axis_index("zero"), o) * z.depth, z.depth)
            term = lax.dot_general(
                routers[o],
                block[0 : z.toks, pl.ds(start, z.depth)],
                (((1,), (1,)), ((), ())),
                preferred_element_type=F32,
            )
            logits = term if logits is None else logits + term
        chosen = number == ids_t[0:1, :]
        for k in range(1, z.topk):
            chosen = chosen | (number == ids_t[k : k + 1, :])
        weights = jnp.where(chosen, jnp.exp(jnp.where(chosen, logits, 0.0)), 0.0)
        gates = weights / jnp.sum(weights, axis=0, keepdims=True)
        marks = slot_marks(z, ids_t)
        mix = []
        for q in range(z.chips):
            gate = jnp.sum(jnp.where(number == served_expert(z, q), gates, 0.0), axis=0, keepdims=True)
            mix.append(marks[q] * gate)
        mix = jnp.concatenate(mix, axis=0).astype(BF16)
        part = z.width // PARTS
        for c in range(PARTS):
            cols = slice(c * part, (c + 1) * part)
            own = slice(b * z.cap, (b + 1) * z.cap)
            y = jnp.concatenate([s[:, cols].astype(F32)[own] for s in backs], axis=0).astype(BF16)
            out[base : base + z.toks, cols] = lax.dot_general(
                mix, y, (((0,), (0,)), ((), ())), preferred_element_type=F32
            ).astype(BF16)


def per_device(tokens, router_weight, expert_ids, gate_weight, up_weight, down_weight):
    layers, near = lax.axis_size("expert"), lax.axis_size("zero")
    z = Sizes(tokens, router_weight.T, expert_ids.T, near, layers)

    def along(array, d):
        return lax.ppermute(array, "expert", [(i, (i + d) % layers) for i in range(layers)])

    def across(array, o):
        return lax.ppermute(array, "zero", [(i, i ^ o) for i in range(near)]) if o else array

    def after(arrays, *others):
        return list(lax.optimization_barrier((*arrays, *others))[: len(arrays)])

    def shape(rows):
        return jax.ShapeDtypeStruct((rows, z.width), BF16)

    def pick(blocks, ride):
        n = len(blocks)
        rows = n * z.cap + (CORES * z.extra if ride else 0)
        return call(functools.partial(pick_kernel, z, n, ride), [shape(rows)] * z.chips, n)(*blocks)

    def arrived(arrays):
        out = jax.ShapeDtypeStruct((8, 128), BF16)
        return call(arrived_kernel, out, len(arrays), flops=PHASE_FLOPS)(*arrays)

    def slabs_across(slabs):
        return [across(s, CORES * q) for q, s in enumerate(slabs)]

    def expert(slabs, n):
        rows = n * z.cap
        return call(
            functools.partial(expert_kernel, z, rows),
            [shape(rows)] * z.chips,
            z.chips + 3,
            [
                pltpu.VMEM((z.chips * rows, z.width), BF16),
                pltpu.VMEM((z.chips * rows, gate_weight.shape[2]), BF16),
            ],
        )(*slabs, gate_weight[0], up_weight[0], down_weight[0])

    def mix(blocks, backs):
        n = len(blocks)
        mine, other = call(
            functools.partial(mix_kernel, z, n), [shape(n // 2 * z.toks)] * 2, n + 2 * z.chips
        )(*blocks, *riders, *backs)
        other = across(other, 1)
        return [
            mine[i * z.toks : (i + 1) * z.toks].astype(F32) + other[i * z.toks : (i + 1) * z.toks].astype(F32)
            for i in range(n // 2)
        ]

    far = layers // 2
    out_turns = list(range(layers))
    back_turns = [far] + [d for d in out_turns if d not in (0, far)] + [0]

    own = call(functools.partial(pad_kernel, z), shape(z.toks + z.extra), 3)(
        tokens, expert_ids.T, router_weight.T
    )

    blocks, pairs, slots, results = {0: own}, {}, {}, {}
    gate = None
    for d in out_turns:
        if d:
            blocks[d] = after([along(blocks[d - 1], 1)], slots[d - 1][1])[0]
        pairs[d] = [blocks[d], across(blocks[d], 1)]
        slabs = pick(pairs[d], d == 1)
        if d:
            seen = slots[d - 1][1:] + ([results[d - 2][0]] if d > 1 else [])
            gate = arrived(seen)
            ready = [after([s], gate)[0] for s in slabs]
            results[d - 1] = expert(after(slots[d - 1], slabs[0]), 2)
        else:
            ready = slabs
        slots[d] = slabs_across(ready)
    riders = slots[1]
    results[d] = expert(after(slots[d], results[d - 1][0]), 2)

    backs, home, leaving = slots[d], {}, {}
    for i, d in enumerate(back_turns):
        first = [leaving[back_turns[i - 2]]] if i > 1 else [results[layers - 2 + i][0]]
        if d == 0:
            first = first + [home[far]]
        rows = [after([r], b, *first)[0] for r, b in zip(results[d], backs)]
        backs = slabs_across(rows)
        last = leaving[back_turns[i - 1]] if i else results[layers - 1][0]
        if d:
            part = mix(pairs[d], after(backs, last))[0]
            leaving[d] = part.astype(BF16)
            way = layers - d
            if d == far:
                home[d] = along(along(leaving[d], way // 2), way - way // 2)
            else:
                home[d] = along(leaving[d], way)
    total = mix(pairs[0], after(backs, last))[0]
    for d in out_turns[1:]:
        total = total + home[d].astype(F32)
    return total.astype(BF16)


def solution(mesh):
    everything = ("expert", "zero")
    in_specs = (
        P(everything, None),
        P("zero", None),
        P(everything, None),
        P(everything, None, None),
        P(everything, None, None),
        P(everything, None, None),
    )
    return jax.shard_map(
        per_device, mesh=mesh, in_specs=in_specs, out_specs=P(everything, None), check_vma=False
    )
```

```python
import functools

import jax
import jax.numpy as jnp
from jax import lax
from jax.experimental import pallas as pl
from jax.experimental.pallas import tpu as pltpu
from jax.sharding import PartitionSpec as P

BF16 = jnp.bfloat16
F32 = jnp.float32
VMEM_LIMIT = 32 * 1024 * 1024
PARTS = 4
CORES = 2
PHASE_FLOPS = 50_000_000_000
VMEM = pl.BlockSpec(memory_space=pltpu.VMEM)


def call(body, out_shape, n_in, scratch=(), flops=1000):
    many = isinstance(out_shape, list)
    return pl.pallas_call(
        body,
        out_shape=out_shape,
        in_specs=[VMEM] * n_in,
        out_specs=[VMEM] * len(out_shape) if many else VMEM,
        scratch_shapes=list(scratch),
        compiler_params=pltpu.CompilerParams(vmem_limit_bytes=VMEM_LIMIT),
        cost_estimate=pl.CostEstimate(flops=flops, bytes_accessed=1000, transcendentals=0),
    )


def arrived_kernel(*refs):
    total = refs[0][0:8, 0:128]
    for ref in refs[1:-1]:
        total = total + ref[0:8, 0:128]
    refs[-1][...] = total


def round_up(n, m):
    return -(-n // m) * m


class Sizes:
    def __init__(self, tokens, router_t, ids_t, near, layers):
        self.toks, self.width = tokens.shape
        self.experts, self.depth = router_t.shape
        self.topk = ids_t.shape[0]
        self.near, self.layers = near, layers
        self.chips = near // CORES
        self.cap = round_up(5 * self.toks * self.topk // (4 * self.experts), 8)
        self.tiles = self.width // self.depth
        self.extra = -(-(1 + self.experts // 8) // self.tiles) * 8
        self.ride = -(-(CORES * self.experts // 8) // self.tiles) * 8

    def tile(self, g):
        r, q = g // self.tiles * 8, g % self.tiles * self.depth
        return slice(r, r + 8), slice(q, q + self.depth)


def pad_kernel(z, tokens_ref, ids_ref, router_ref, out):
    out[0 : z.toks, :] = tokens_ref[...]
    blank = jnp.zeros((z.extra, z.width), BF16)
    out[z.toks : z.toks + z.extra, :] = blank
    out[z.toks : z.toks + 8, 0 : z.toks] = ids_ref[...].astype(F32).astype(BF16)
    for g in range(z.experts // 8):
        rows, cols = z.tile(g + 1)
        out[z.toks + rows.start : z.toks + rows.stop, cols] = router_ref[8 * g : 8 * g + 8, :]


def served_expert(z, q):
    return lax.axis_index("expert") * z.near + lax.bitwise_xor(lax.axis_index("zero"), q * CORES)


def ids_of(z, block_ref):
    return block_ref[z.toks : z.toks + 8, 0 : z.toks].astype(F32).astype(jnp.int32)


def slot_marks(z, ids_t):
    has = jnp.concatenate(
        [
            jnp.max((ids_t == served_expert(z, q)).astype(F32), axis=0, keepdims=True)
            for q in range(z.chips)
        ]
        * 2,
        axis=0,
    )
    earlier = (
        lax.broadcasted_iota(jnp.int32, (z.toks, z.toks), 0)
        < lax.broadcasted_iota(jnp.int32, (z.toks, z.toks), 1)
    ).astype(F32).astype(BF16)
    slot = jnp.dot(has.astype(BF16), earlier, preferred_element_type=F32)
    slot = jnp.where(has > 0, slot, -1.0)
    row = lax.broadcasted_iota(jnp.int32, (z.cap, z.toks), 0).astype(F32)
    return [jnp.where(row == slot[q : q + 1, :], 1.0, 0.0) for q in range(z.chips)]


def pick_kernel(z, n, ride, *refs):
    blocks, outs = refs[:n], refs[n:]
    marks = [jnp.concatenate(slot_marks(z, ids_of(z, b)), axis=0).astype(BF16) for b in blocks]
    part = z.width // PARTS
    for c in range(PARTS):
        cols = slice(c * part, (c + 1) * part)
        rows = [jnp.dot(m, b[0 : z.toks, cols], preferred_element_type=F32) for m, b in zip(marks, blocks)]
        for q in range(z.chips):
            mine = [r[q * z.cap : (q + 1) * z.cap] for r in rows]
            outs[q][0 : n * z.cap, cols] = jnp.concatenate(mine, axis=0).astype(BF16)
    if ride:
        for r in range(CORES):
            for g in range(z.experts // 8):
                rows, cols = z.tile(g + 1)
                piece = blocks[r][z.toks + rows.start : z.toks + rows.stop, cols]
                rows, cols = z.tile(r * (z.experts // 8) + g)
                for q in range(z.chips):
                    outs[q][n * z.cap + rows.start : n * z.cap + rows.stop, cols] = piece


def expert_kernel(z, rows, *refs):
    slabs, gate_ref, up_ref, down_ref = refs[: z.chips], *refs[z.chips : z.chips + 3]
    outs, (x, hidden) = refs[z.chips + 3 : 2 * z.chips + 3], refs[2 * z.chips + 3 :]
    for q in range(z.chips):
        x[q * rows : (q + 1) * rows, :] = slabs[q][0:rows, :]
    ff = gate_ref.shape[1]
    tile = 256
    for f in range(0, ff, tile):
        gate = jnp.dot(x[...], gate_ref[:, f : f + tile], preferred_element_type=F32)
        upper = jnp.dot(x[...], up_ref[:, f : f + tile], preferred_element_type=F32)
        hidden[:, f : f + tile] = (gate / (1.0 + jnp.exp(-gate)) * upper).astype(BF16)
    for c in range(0, z.width, tile):
        y = jnp.dot(hidden[...], down_ref[:, c : c + tile], preferred_element_type=F32)
        for q in range(z.chips):
            outs[q][:, c : c + tile] = y[q * rows : (q + 1) * rows].astype(BF16)


def mix_kernel(z, n, *refs):
    blocks, refs = refs[:n], refs[n:]
    riders, backs, outs = refs[: z.chips], refs[z.chips : 2 * z.chips], refs[2 * z.chips :]
    number = lax.broadcasted_iota(jnp.int32, (z.experts, z.toks), 0)
    routers = []
    for q in range(z.chips):
        for r in range(CORES):
            base = CORES * z.cap
            pieces = []
            for g in range(z.experts // 8):
                rows, cols = z.tile(r * (z.experts // 8) + g)
                pieces.append(riders[q][base + rows.start : base + rows.stop, cols].astype(F32))
            routers.append(jnp.concatenate(pieces, axis=0).astype(BF16))
    for b, block in enumerate(blocks):
        ids_t = ids_of(z, block)
        logits = None
        for o in range(z.near):
            start = pl.multiple_of(lax.bitwise_xor(lax.axis_index("zero"), o) * z.depth, z.depth)
            term = lax.dot_general(
                routers[o],
                block[0 : z.toks, pl.ds(start, z.depth)],
                (((1,), (1,)), ((), ())),
                preferred_element_type=F32,
            )
            logits = term if logits is None else logits + term
        chosen = number == ids_t[0:1, :]
        for k in range(1, z.topk):
            chosen = chosen | (number == ids_t[k : k + 1, :])
        weights = jnp.where(chosen, jnp.exp(jnp.where(chosen, logits, 0.0)), 0.0)
        gates = weights / jnp.sum(weights, axis=0, keepdims=True)
        marks = slot_marks(z, ids_t)
        mix = []
        for q in range(z.chips):
            gate = jnp.sum(jnp.where(number == served_expert(z, q), gates, 0.0), axis=0, keepdims=True)
            mix.append(marks[q] * gate)
        mix = jnp.concatenate(mix, axis=0).astype(BF16)
        part = z.width // PARTS
        for c in range(PARTS):
            cols = slice(c * part, (c + 1) * part)
            own = slice(b * z.cap, (b + 1) * z.cap)
            y = jnp.concatenate([s[:, cols].astype(F32)[own] for s in backs], axis=0).astype(BF16)
            mixed = lax.dot_general(mix, y, (((0,), (0,)), ((), ())), preferred_element_type=F32).astype(BF16)
            if b == 0:
                outs[0][:, cols] = mixed
            else:
                half = z.toks // 2
                outs[1][:, cols] = mixed[0:half]
                outs[2][:, cols] = mixed[half:]


def join_kernel(*refs):
    out = refs[-1]
    half = out.shape[0] // 2
    for i in range(2):
        rows = slice(i * half, (i + 1) * half)
        total = refs[0][rows, :].astype(F32) + refs[1 + i][...].astype(F32)
        for ref in refs[3:-1]:
            total = total + ref[rows, :].astype(F32)
        out[rows, :] = total.astype(BF16)


def per_device(tokens, router_weight, expert_ids, gate_weight, up_weight, down_weight):
    layers, near = lax.axis_size("expert"), lax.axis_size("zero")
    z = Sizes(tokens, router_weight.T, expert_ids.T, near, layers)

    def along(array, d):
        return lax.ppermute(array, "expert", [(i, (i + d) % layers) for i in range(layers)])

    def across(array, o):
        return lax.ppermute(array, "zero", [(i, i ^ o) for i in range(near)]) if o else array

    def after(arrays, *others):
        return list(lax.optimization_barrier((*arrays, *others))[: len(arrays)])

    def shape(rows):
        return jax.ShapeDtypeStruct((rows, z.width), BF16)

    def pick(blocks, ride):
        n = len(blocks)
        rows = n * z.cap + (z.ride if ride else 0)
        return call(functools.partial(pick_kernel, z, n, ride), [shape(rows)] * z.chips, n)(*blocks)

    def arrived(arrays):
        out = jax.ShapeDtypeStruct((8, 128), BF16)
        return call(arrived_kernel, out, len(arrays), flops=PHASE_FLOPS)(*arrays)

    def slabs_across(slabs):
        return [across(s, CORES * q) for q, s in enumerate(slabs)]

    def expert(slabs, n):
        rows = n * z.cap
        return call(
            functools.partial(expert_kernel, z, rows),
            [shape(rows)] * z.chips,
            z.chips + 3,
            [
                pltpu.VMEM((z.chips * rows, z.width), BF16),
                pltpu.VMEM((z.chips * rows, gate_weight.shape[2]), BF16),
            ],
        )(*slabs, gate_weight[0], up_weight[0], down_weight[0])

    def mix(blocks, backs):
        mine, *other = call(
            functools.partial(mix_kernel, z, CORES),
            [shape(z.toks), shape(z.toks // 2), shape(z.toks // 2)],
            CORES + 2 * z.chips,
            flops=PHASE_FLOPS,
        )(*blocks, *riders, *backs)
        return [mine] + [across(part, 1) for part in other]

    def join(parts):
        return call(join_kernel, shape(z.toks), len(parts))(*parts)

    far = layers // 2
    out_turns = list(range(layers))
    back_turns = [far] + [d for d in out_turns if d not in (0, far)] + [0]

    own = call(functools.partial(pad_kernel, z), shape(z.toks + z.extra), 3)(
        tokens, expert_ids.T, router_weight.T
    )

    blocks, pairs, slots, results = {0: own}, {}, {}, {}
    for d in out_turns:
        if d:
            blocks[d] = after([along(blocks[d - 1], 1)], slots[d - 1][1])[0]
        pairs[d] = [blocks[d], across(blocks[d], 1)]
        slabs = pick(pairs[d], d == 1)
        ready = slabs
        if d:
            gate = arrived(slots[d - 1][1:] + ([results[d - 2][0]] if d > 1 else []))
            ready = [after([s], gate)[0] for s in slabs]
            results[d - 1] = expert(after(slots[d - 1], slabs[0]), 2)
        slots[d] = slabs_across(ready)
    riders = slots[1]
    results[d] = expert(after(slots[d], results[d - 1][0]), 2)

    backs, home, leaving = slots[d], {}, {}
    for i, d in enumerate(back_turns):
        first = [leaving[back_turns[i - 2]]] if i > 1 else [results[layers - 2 + i][0]]
        if d == 0:
            first = first + [home[far]]
        rows = [after([r], b, *first)[0] for r, b in zip(results[d], backs)]
        backs = slabs_across(rows)
        last = leaving[back_turns[i - 1]] if i else results[layers - 1][0]
        sums = mix(pairs[d], after(backs, last))
        if d:
            leaving[d] = join(sums)
            way = layers - d
            if d == far:
                home[d] = along(along(leaving[d], way // 2), way - way // 2)
            else:
                home[d] = along(leaving[d], way)
    return join(sums + [home[d] for d in out_turns[1:]])


def solution(mesh):
    everything = ("expert", "zero")
    in_specs = (
        P(everything, None),
        P("zero", None),
        P(everything, None),
        P(everything, None, None),
        P(everything, None, None),
        P(everything, None, None),
    )
    return jax.shard_map(
        per_device, mesh=mesh, in_specs=in_specs, out_specs=P(everything, None), check_vma=False
    )
```

```python
import functools

import jax
import jax.numpy as jnp
from jax import lax
from jax.experimental import pallas as pl
from jax.experimental.pallas import tpu as pltpu
from jax.sharding import PartitionSpec as P

BF16 = jnp.bfloat16
F32 = jnp.float32
VMEM_LIMIT = 32 * 1024 * 1024
PARTS = 4
CORES = 2
PHASE_FLOPS = 50_000_000_000
VMEM = pl.BlockSpec(memory_space=pltpu.VMEM)


def call(body, out_shape, n_in, scratch=(), flops=1000):
    many = isinstance(out_shape, list)
    return pl.pallas_call(
        body,
        out_shape=out_shape,
        in_specs=[VMEM] * n_in,
        out_specs=[VMEM] * len(out_shape) if many else VMEM,
        scratch_shapes=list(scratch),
        compiler_params=pltpu.CompilerParams(vmem_limit_bytes=VMEM_LIMIT),
        cost_estimate=pl.CostEstimate(flops=flops, bytes_accessed=1000, transcendentals=0),
    )


def arrived_kernel(*refs):
    total = refs[0][0:8, 0:128]
    for ref in refs[1:-1]:
        total = total + ref[0:8, 0:128]
    refs[-1][...] = total


def round_up(n, m):
    return -(-n // m) * m


class Sizes:
    def __init__(self, tokens, router_t, ids_t, near, layers):
        self.toks, self.width = tokens.shape
        self.experts, self.depth = router_t.shape
        self.topk = ids_t.shape[0]
        self.near, self.layers = near, layers
        self.chips = near // CORES
        self.cap = round_up(5 * self.toks * self.topk // (4 * self.experts), 8)
        self.tiles = self.width // self.depth
        self.extra = -(-(1 + self.experts // 8) // self.tiles) * 8
        self.ride = -(-(CORES * self.experts // 8) // self.tiles) * 8

    def tile(self, g):
        r, q = g // self.tiles * 8, g % self.tiles * self.depth
        return slice(r, r + 8), slice(q, q + self.depth)


def pad_kernel(z, tokens_ref, ids_ref, router_ref, out):
    out[0 : z.toks, :] = tokens_ref[...]
    blank = jnp.zeros((z.extra, z.width), BF16)
    out[z.toks : z.toks + z.extra, :] = blank
    out[z.toks : z.toks + 8, 0 : z.toks] = ids_ref[...].astype(F32).astype(BF16)
    for g in range(z.experts // 8):
        rows, cols = z.tile(g + 1)
        out[z.toks + rows.start : z.toks + rows.stop, cols] = router_ref[8 * g : 8 * g + 8, :]


def served_expert(z, q):
    return lax.axis_index("expert") * z.near + lax.bitwise_xor(lax.axis_index("zero"), q * CORES)


def ids_of(z, block_ref):
    return block_ref[z.toks : z.toks + 8, 0 : z.toks].astype(F32).astype(jnp.int32)


def slot_marks(z, ids_t):
    has = jnp.concatenate(
        [
            jnp.max((ids_t == served_expert(z, q)).astype(F32), axis=0, keepdims=True)
            for q in range(z.chips)
        ]
        * 2,
        axis=0,
    )
    earlier = (
        lax.broadcasted_iota(jnp.int32, (z.toks, z.toks), 0)
        < lax.broadcasted_iota(jnp.int32, (z.toks, z.toks), 1)
    ).astype(F32).astype(BF16)
    slot = jnp.dot(has.astype(BF16), earlier, preferred_element_type=F32)
    slot = jnp.where(has > 0, slot, -1.0)
    row = lax.broadcasted_iota(jnp.int32, (z.cap, z.toks), 0).astype(F32)
    return [jnp.where(row == slot[q : q + 1, :], 1.0, 0.0) for q in range(z.chips)]


def pick_kernel(z, n, ride, *refs):
    blocks, outs = refs[:n], refs[n:]
    marks = [jnp.concatenate(slot_marks(z, ids_of(z, b)), axis=0).astype(BF16) for b in blocks]
    part = z.width // PARTS
    for c in range(PARTS):
        cols = slice(c * part, (c + 1) * part)
        rows = [jnp.dot(m, b[0 : z.toks, cols], preferred_element_type=F32) for m, b in zip(marks, blocks)]
        for q in range(z.chips):
            mine = [r[q * z.cap : (q + 1) * z.cap] for r in rows]
            outs[q][0 : n * z.cap, cols] = jnp.concatenate(mine, axis=0).astype(BF16)
    if ride:
        for r in range(CORES):
            for g in range(z.experts // 8):
                rows, cols = z.tile(g + 1)
                piece = blocks[r][z.toks + rows.start : z.toks + rows.stop, cols]
                rows, cols = z.tile(r * (z.experts // 8) + g)
                for q in range(z.chips):
                    outs[q][n * z.cap + rows.start : n * z.cap + rows.stop, cols] = piece


def expert_kernel(z, rows, *refs):
    slabs, gate_ref, up_ref, down_ref = refs[: z.chips], *refs[z.chips : z.chips + 3]
    outs, (x, hidden) = refs[z.chips + 3 : 2 * z.chips + 3], refs[2 * z.chips + 3 :]
    for q in range(z.chips):
        x[q * rows : (q + 1) * rows, :] = slabs[q][0:rows, :]
    ff = gate_ref.shape[1]
    tile = 256
    for f in range(0, ff, tile):
        gate = jnp.dot(x[...], gate_ref[:, f : f + tile], preferred_element_type=F32)
        upper = jnp.dot(x[...], up_ref[:, f : f + tile], preferred_element_type=F32)
        hidden[:, f : f + tile] = (gate / (1.0 + jnp.exp(-gate)) * upper).astype(BF16)
    for c in range(0, z.width, tile):
        y = jnp.dot(hidden[...], down_ref[:, c : c + tile], preferred_element_type=F32)
        for q in range(z.chips):
            outs[q][:, c : c + tile] = y[q * rows : (q + 1) * rows].astype(BF16)


def mix_kernel(z, n, *refs):
    blocks, refs = refs[:n], refs[n:]
    riders, backs, outs = refs[: z.chips], refs[z.chips : 2 * z.chips], refs[2 * z.chips :]
    number = lax.broadcasted_iota(jnp.int32, (z.experts, z.toks), 0)
    routers = []
    for q in range(z.chips):
        for r in range(CORES):
            base = CORES * z.cap
            pieces = []
            for g in range(z.experts // 8):
                rows, cols = z.tile(r * (z.experts // 8) + g)
                pieces.append(riders[q][base + rows.start : base + rows.stop, cols].astype(F32))
            routers.append(jnp.concatenate(pieces, axis=0).astype(BF16))
    for b, block in enumerate(blocks):
        ids_t = ids_of(z, block)
        logits = None
        for o in range(z.near):
            start = pl.multiple_of(lax.bitwise_xor(lax.axis_index("zero"), o) * z.depth, z.depth)
            term = lax.dot_general(
                routers[o],
                block[0 : z.toks, pl.ds(start, z.depth)],
                (((1,), (1,)), ((), ())),
                preferred_element_type=F32,
            )
            logits = term if logits is None else logits + term
        chosen = number == ids_t[0:1, :]
        for k in range(1, z.topk):
            chosen = chosen | (number == ids_t[k : k + 1, :])
        weights = jnp.where(chosen, jnp.exp(jnp.where(chosen, logits, 0.0)), 0.0)
        gates = weights / jnp.sum(weights, axis=0, keepdims=True)
        marks = slot_marks(z, ids_t)
        mix = []
        for q in range(z.chips):
            gate = jnp.sum(jnp.where(number == served_expert(z, q), gates, 0.0), axis=0, keepdims=True)
            mix.append(marks[q] * gate)
        mix = jnp.concatenate(mix, axis=0).astype(BF16)
        part = z.width // PARTS
        for c in range(PARTS):
            cols = slice(c * part, (c + 1) * part)
            own = slice(b * z.cap, (b + 1) * z.cap)
            y = jnp.concatenate([s[:, cols].astype(F32)[own] for s in backs], axis=0).astype(BF16)
            mixed = lax.dot_general(mix, y, (((0,), (0,)), ((), ())), preferred_element_type=F32).astype(BF16)
            if b == 0:
                outs[0][:, cols] = mixed
            else:
                half = z.toks // 2
                outs[1][:, cols] = mixed[0:half]
                outs[2][:, cols] = mixed[half:]


def join_kernel(*refs):
    out = refs[-1]
    half = out.shape[0] // 2
    for i in range(2):
        rows = slice(i * half, (i + 1) * half)
        total = refs[0][rows, :].astype(F32) + refs[1 + i][...].astype(F32)
        for ref in refs[3:-1]:
            total = total + ref[rows, :].astype(F32)
        out[rows, :] = total.astype(BF16)


def per_device(tokens, router_weight, expert_ids, gate_weight, up_weight, down_weight):
    layers, near = lax.axis_size("expert"), lax.axis_size("zero")
    z = Sizes(tokens, router_weight.T, expert_ids.T, near, layers)

    def along(array, d):
        return lax.ppermute(array, "expert", [(i, (i + d) % layers) for i in range(layers)])

    def across(array, o):
        return lax.ppermute(array, "zero", [(i, i ^ o) for i in range(near)]) if o else array

    def after(arrays, *others):
        return list(lax.optimization_barrier((*arrays, *others))[: len(arrays)])

    def shape(rows):
        return jax.ShapeDtypeStruct((rows, z.width), BF16)

    def pick(blocks, ride, flops=1000):
        n = len(blocks)
        rows = n * z.cap + (z.ride if ride else 0)
        body = functools.partial(pick_kernel, z, n, ride)
        return call(body, [shape(rows)] * z.chips, n, flops=flops)(*blocks)

    def arrived(arrays):
        out = jax.ShapeDtypeStruct((8, 128), BF16)
        return call(arrived_kernel, out, len(arrays), flops=PHASE_FLOPS)(*arrays)

    def slabs_across(slabs):
        return [across(s, CORES * q) for q, s in enumerate(slabs)]

    def expert(slabs, n, flops=1000):
        rows = n * z.cap
        return call(
            functools.partial(expert_kernel, z, rows),
            [shape(rows)] * z.chips,
            z.chips + 3,
            [
                pltpu.VMEM((z.chips * rows, z.width), BF16),
                pltpu.VMEM((z.chips * rows, gate_weight.shape[2]), BF16),
            ],
            flops,
        )(*slabs, gate_weight[0], up_weight[0], down_weight[0])

    def mix(blocks, backs):
        riders = slots[1]
        mine, *other = call(
            functools.partial(mix_kernel, z, CORES),
            [shape(z.toks), shape(z.toks // 2), shape(z.toks // 2)],
            CORES + 2 * z.chips,
            flops=PHASE_FLOPS,
        )(*blocks, *riders, *backs)
        return [mine] + [across(part, 1) for part in other]

    def join(parts):
        return call(join_kernel, shape(z.toks), len(parts))(*parts)

    own = call(functools.partial(pad_kernel, z), shape(z.toks + z.extra), 3)(
        tokens, expert_ids.T, router_weight.T
    )

    end = layers - 1
    turns = [(d, True) for d in range(end)] + [(d, False) for d in range(1, end)]
    turns += [(end, True), (end, False), (0, False)]
    blocks, pairs, slots, results = {0: own}, {}, {}, {}
    leaving, home, seen, waiting = {}, {}, None, None
    for d, outward in turns:
        if outward:
            if d:
                blocks[d] = after([along(blocks[d - 1], 1)], slots[d - 1][1])[0]
            pairs[d] = [blocks[d], across(blocks[d], 1)]
            rows = slabs = pick(pairs[d], d == 1, PHASE_FLOPS if d == end else 1000)
            if 0 < d < end:
                gate = arrived(slots[d - 1][1:] + ([results[d - 2][0]] if d > 1 else []))
                rows = [after([s], gate)[0] for s in slabs]
                results[d - 1] = expert(after(slots[d - 1], slabs[0]), 2)
            if d == end:
                rows = [after([r], b)[0] for r, b in zip(slabs, seen)]
            seen = slots[d] = slabs_across(rows)
            if d == end - 1:
                results[d] = expert(slots[d], 2)
            if d == end:
                first = [leaving[e] for e in range(1, end)]
                results[d] = expert(after(slots[d], *first), 2, PHASE_FLOPS)
        else:
            rows = [after([r], b)[0] for r, b in zip(results[d], seen)]
            seen = backs = slabs_across(rows)
            first = [(home if d else leaving)[waiting]] if waiting else [results[end - 1][0]]
            sums = mix(pairs[d], after(backs, *first))
            if d:
                leaving[d] = join(sums)
                home[d] = along(leaving[d], layers - d)
                waiting = d
    return join(sums + [home[d] for d in range(1, layers)])


def solution(mesh):
    everything = ("expert", "zero")
    in_specs = (
        P(everything, None),
        P("zero", None),
        P(everything, None),
        P(everything, None, None),
        P(everything, None, None),
        P(everything, None, None),
    )
    return jax.shard_map(
        per_device, mesh=mesh, in_specs=in_specs, out_specs=P(everything, None), check_vma=False
    )
```

```python
import functools

import jax
import jax.numpy as jnp
from jax import lax
from jax.experimental import pallas as pl
from jax.experimental.pallas import tpu as pltpu
from jax.sharding import PartitionSpec as P

BF16 = jnp.bfloat16
F32 = jnp.float32
VMEM_LIMIT = 32 * 1024 * 1024
PAD_VMEM_LIMIT = 60 * 1024 * 1024
PARTS = 4
CORES = 2
PHASE_FLOPS = 50_000_000_000
VMEM = pl.BlockSpec(memory_space=pltpu.VMEM)


def call(body, out_shape, n_in, scratch=(), flops=1000, spec=VMEM, limit=VMEM_LIMIT):
    many = isinstance(out_shape, list)
    return pl.pallas_call(
        body,
        out_shape=out_shape,
        in_specs=[spec] * n_in,
        out_specs=[VMEM] * len(out_shape) if many else VMEM,
        scratch_shapes=list(scratch),
        compiler_params=pltpu.CompilerParams(vmem_limit_bytes=limit),
        cost_estimate=pl.CostEstimate(flops=flops, bytes_accessed=1000, transcendentals=0),
    )


def arrived_kernel(*refs):
    total = refs[0][0:8, 0:128]
    for ref in refs[1:-1]:
        total = total + ref[0:8, 0:128]
    refs[-1][...] = total


def round_up(n, m):
    return -(-n // m) * m


class Sizes:
    def __init__(self, tokens, router_t, ids_t, near, layers):
        self.toks, self.width = tokens.shape
        self.experts, self.depth = router_t.shape
        self.topk = ids_t.shape[0]
        self.near, self.layers = near, layers
        self.chips = near // CORES
        self.offsets = sorted(range(self.chips), key=lambda q: (q == 2, q))
        self.cap = round_up(5 * self.toks * self.topk // (4 * self.experts), 8)
        self.tiles = self.width // self.depth
        self.extra = -(-(1 + self.experts // 8) // self.tiles) * 8
        self.ride = -(-(CORES * self.experts // 8) // self.tiles) * 8

    def tile(self, g):
        r, q = g // self.tiles * 8, g % self.tiles * self.depth
        return slice(r, r + 8), slice(q, q + self.depth)


def pad_kernel(z, tokens_ref, ids_ref, router_ref, out, ids, router, sems):
    copies = [
        pltpu.make_async_copy(tokens_ref, out.at[0 : z.toks, :], sems.at[0]),
        pltpu.make_async_copy(ids_ref, ids, sems.at[1]),
        pltpu.make_async_copy(router_ref, router, sems.at[2]),
    ]
    for copy in copies:
        copy.start()
    out[z.toks : z.toks + z.extra, :] = jnp.zeros((z.extra, z.width), BF16)
    for copy in copies[1:]:
        copy.wait()
    out[z.toks : z.toks + 8, 0 : z.toks] = ids[...].astype(F32).astype(BF16)
    for g in range(z.experts // 8):
        rows, cols = z.tile(g + 1)
        out[z.toks + rows.start : z.toks + rows.stop, cols] = router[8 * g : 8 * g + 8, :]
    copies[0].wait()


def served_expert(z, q):
    return lax.axis_index("expert") * z.near + lax.bitwise_xor(lax.axis_index("zero"), q * CORES)


def ids_of(z, block_ref):
    return block_ref[z.toks : z.toks + 8, 0 : z.toks].astype(F32).astype(jnp.int32)


def slot_marks(z, ids_t):
    has = jnp.concatenate(
        [
            jnp.max((ids_t == served_expert(z, q)).astype(F32), axis=0, keepdims=True)
            for q in z.offsets
        ]
        * 2,
        axis=0,
    )
    earlier = (
        lax.broadcasted_iota(jnp.int32, (z.toks, z.toks), 0)
        < lax.broadcasted_iota(jnp.int32, (z.toks, z.toks), 1)
    ).astype(F32).astype(BF16)
    slot = jnp.dot(has.astype(BF16), earlier, preferred_element_type=F32)
    slot = jnp.where(has > 0, slot, -1.0)
    row = lax.broadcasted_iota(jnp.int32, (z.cap, z.toks), 0).astype(F32)
    return [jnp.where(row == slot[q : q + 1, :], 1.0, 0.0) for q in range(z.chips)]


def pick_kernel(z, n, ride, *refs):
    blocks, outs = refs[:n], refs[n:]
    marks = [jnp.concatenate(slot_marks(z, ids_of(z, b)), axis=0).astype(BF16) for b in blocks]
    part = z.width // PARTS
    for c in range(PARTS):
        cols = slice(c * part, (c + 1) * part)
        rows = [jnp.dot(m, b[0 : z.toks, cols], preferred_element_type=F32) for m, b in zip(marks, blocks)]
        for q in range(z.chips):
            mine = [r[q * z.cap : (q + 1) * z.cap] for r in rows]
            outs[q][0 : n * z.cap, cols] = jnp.concatenate(mine, axis=0).astype(BF16)
    if ride:
        for r in range(CORES):
            for g in range(z.experts // 8):
                rows, cols = z.tile(g + 1)
                piece = blocks[r][z.toks + rows.start : z.toks + rows.stop, cols]
                rows, cols = z.tile(r * (z.experts // 8) + g)
                for q in range(z.chips):
                    outs[q][n * z.cap + rows.start : n * z.cap + rows.stop, cols] = piece


def expert_kernel(z, rows, *refs):
    slabs, gate_ref, up_ref, down_ref = refs[: z.chips], *refs[z.chips : z.chips + 3]
    outs, (x, hidden) = refs[z.chips + 3 : 2 * z.chips + 3], refs[2 * z.chips + 3 :]
    for q in range(z.chips):
        x[q * rows : (q + 1) * rows, :] = slabs[q][0:rows, :]
    ff = gate_ref.shape[1]
    tile = 256
    for f in range(0, ff, tile):
        gate = jnp.dot(x[...], gate_ref[:, f : f + tile], preferred_element_type=F32)
        upper = jnp.dot(x[...], up_ref[:, f : f + tile], preferred_element_type=F32)
        hidden[:, f : f + tile] = (gate / (1.0 + jnp.exp(-gate)) * upper).astype(BF16)
    for c in range(0, z.width, tile):
        y = jnp.dot(hidden[...], down_ref[:, c : c + tile], preferred_element_type=F32)
        for q in range(z.chips):
            outs[q][:, c : c + tile] = y[q * rows : (q + 1) * rows].astype(BF16)


def mix_kernel(z, n, *refs):
    blocks, refs = refs[:n], refs[n:]
    riders, backs, outs = refs[: z.chips], refs[z.chips : 2 * z.chips], refs[2 * z.chips :]
    number = lax.broadcasted_iota(jnp.int32, (z.experts, z.toks), 0)
    routers = {}
    for i, q in enumerate(z.offsets):
        for r in range(CORES):
            base = CORES * z.cap
            pieces = []
            for g in range(z.experts // 8):
                rows, cols = z.tile(r * (z.experts // 8) + g)
                pieces.append(riders[i][base + rows.start : base + rows.stop, cols].astype(F32))
            routers[CORES * q + r] = jnp.concatenate(pieces, axis=0).astype(BF16)
    for b, block in enumerate(blocks):
        ids_t = ids_of(z, block)
        logits = None
        for o in range(z.near):
            start = pl.multiple_of(lax.bitwise_xor(lax.axis_index("zero"), o) * z.depth, z.depth)
            term = lax.dot_general(
                routers[o],
                block[0 : z.toks, pl.ds(start, z.depth)],
                (((1,), (1,)), ((), ())),
                preferred_element_type=F32,
            )
            logits = term if logits is None else logits + term
        chosen = number == ids_t[0:1, :]
        for k in range(1, z.topk):
            chosen = chosen | (number == ids_t[k : k + 1, :])
        weights = jnp.where(chosen, jnp.exp(jnp.where(chosen, logits, 0.0)), 0.0)
        gates = weights / jnp.sum(weights, axis=0, keepdims=True)
        marks = slot_marks(z, ids_t)
        mix = []
        for i, q in enumerate(z.offsets):
            gate = jnp.sum(jnp.where(number == served_expert(z, q), gates, 0.0), axis=0, keepdims=True)
            mix.append(marks[i] * gate)
        mix = jnp.concatenate(mix, axis=0).astype(BF16)
        part = z.width // PARTS
        for c in range(PARTS):
            cols = slice(c * part, (c + 1) * part)
            own = slice(b * z.cap, (b + 1) * z.cap)
            y = jnp.concatenate([s[:, cols].astype(F32)[own] for s in backs], axis=0).astype(BF16)
            mixed = lax.dot_general(mix, y, (((0,), (0,)), ((), ())), preferred_element_type=F32).astype(BF16)
            if b == 0:
                outs[0][:, cols] = mixed
            else:
                half = z.toks // 2
                outs[1][:, cols] = mixed[0:half]
                outs[2][:, cols] = mixed[half:]


def join_kernel(*refs):
    out = refs[-1]
    half = out.shape[0] // 2
    for i in range(2):
        rows = slice(i * half, (i + 1) * half)
        total = refs[0][rows, :].astype(F32) + refs[1 + i][...].astype(F32)
        for ref in refs[3:-1]:
            total = total + ref[rows, :].astype(F32)
        out[rows, :] = total.astype(BF16)


def per_device(tokens, router_weight, expert_ids, gate_weight, up_weight, down_weight):
    layers, near = lax.axis_size("expert"), lax.axis_size("zero")
    z = Sizes(tokens, router_weight.T, expert_ids.T, near, layers)

    def along(array, d):
        return lax.ppermute(array, "expert", [(i, (i + d) % layers) for i in range(layers)])

    def across(array, o):
        return lax.ppermute(array, "zero", [(i, i ^ o) for i in range(near)]) if o else array

    def after(arrays, *others):
        return list(lax.optimization_barrier((*arrays, *others))[: len(arrays)])

    def shape(rows):
        return jax.ShapeDtypeStruct((rows, z.width), BF16)

    def pick(blocks, ride, flops=1000):
        n = len(blocks)
        rows = n * z.cap + (z.ride if ride else 0)
        body = functools.partial(pick_kernel, z, n, ride)
        return call(body, [shape(rows)] * z.chips, n, flops=flops)(*blocks)

    def arrived(arrays):
        out = jax.ShapeDtypeStruct((8, 128), BF16)
        return call(arrived_kernel, out, len(arrays), flops=PHASE_FLOPS)(*arrays)

    def slabs_across(slabs):
        return [across(s, CORES * q) for q, s in zip(z.offsets, slabs)]

    def expert(slabs, n, flops=1000):
        rows = n * z.cap
        return call(
            functools.partial(expert_kernel, z, rows),
            [shape(rows)] * z.chips,
            z.chips + 3,
            [
                pltpu.VMEM((z.chips * rows, z.width), BF16),
                pltpu.VMEM((z.chips * rows, gate_weight.shape[2]), BF16),
            ],
            flops,
        )(*slabs, gate_weight[0], up_weight[0], down_weight[0])

    def mix(blocks, backs):
        riders = slots[1]
        mine, *other = call(
            functools.partial(mix_kernel, z, CORES),
            [shape(z.toks), shape(z.toks // 2), shape(z.toks // 2)],
            CORES + 2 * z.chips,
            flops=PHASE_FLOPS,
        )(*blocks, *riders, *backs)
        return [mine] + [across(part, 1) for part in other]

    def join(parts):
        return call(join_kernel, shape(z.toks), len(parts))(*parts)

    own = call(
        functools.partial(pad_kernel, z),
        shape(z.toks + z.extra),
        3,
        [
            pltpu.VMEM((z.topk, z.toks), jnp.int32),
            pltpu.VMEM((z.experts, z.depth), BF16),
            pltpu.SemaphoreType.DMA((3,)),
        ],
        spec=pl.BlockSpec(memory_space=pl.ANY),
        limit=PAD_VMEM_LIMIT,
    )(tokens, expert_ids.T, router_weight.T)

    end = layers - 1
    turns = [(d, True) for d in range(end)] + [(d, False) for d in range(1, end)]
    turns += [(end, True), (end, False), (0, False)]
    blocks, pairs, slots, results = {0: own}, {}, {}, {}
    leaving, home, seen, waiting = {}, {}, None, None
    for d, outward in turns:
        if outward:
            if d:
                blocks[d] = after([along(blocks[d - 1], 1)], slots[d - 1][1])[0]
            pairs[d] = [blocks[d], across(blocks[d], 1)]
            rows = slabs = pick(pairs[d], d == 1, PHASE_FLOPS if d == end else 1000)
            if 0 < d < end:
                gate = arrived(slots[d - 1][1:] + ([results[d - 2][0]] if d > 1 else []))
                rows = [after([s], gate)[0] for s in slabs]
                results[d - 1] = expert(after(slots[d - 1], slabs[0]), 2)
            if d == end:
                rows = [after([r], b)[0] for r, b in zip(slabs, seen)]
            seen = slots[d] = slabs_across(rows)
            if d == end - 1:
                results[d] = expert(slots[d], 2)
            if d == end:
                first = [leaving[e] for e in range(1, end)]
                results[d] = expert(after(slots[d], *first), 2, PHASE_FLOPS)
        else:
            rows = [after([r], b)[0] for r, b in zip(results[d], seen)]
            seen = backs = slabs_across(rows)
            first = [(home if d else leaving)[waiting]] if waiting else [results[end - 1][0]]
            sums = mix(pairs[d], after(backs, *first))
            if d:
                leaving[d] = join(sums)
                home[d] = along(leaving[d], layers - d)
                waiting = d
    return join(sums + [home[d] for d in range(1, layers)])


def solution(mesh):
    everything = ("expert", "zero")
    in_specs = (
        P(everything, None),
        P("zero", None),
        P(everything, None),
        P(everything, None, None),
        P(everything, None, None),
        P(everything, None, None),
    )
    return jax.shard_map(
        per_device, mesh=mesh, in_specs=in_specs, out_specs=P(everything, None), check_vma=False
    )
```

```python
import functools

import jax
import jax.numpy as jnp
from jax import lax
from jax.experimental import pallas as pl
from jax.experimental.pallas import tpu as pltpu
from jax.sharding import PartitionSpec as P

BF16 = jnp.bfloat16
F32 = jnp.float32
VMEM_LIMIT = 32 * 1024 * 1024
PAD_VMEM_LIMIT = 60 * 1024 * 1024
PARTS = 4
CORES = 2
PHASE_FLOPS = 50_000_000_000
VMEM = pl.BlockSpec(memory_space=pltpu.VMEM)


def call(body, out_shape, n_in, scratch=(), flops=1000, spec=VMEM, limit=VMEM_LIMIT):
    many = isinstance(out_shape, list)
    return pl.pallas_call(
        body,
        out_shape=out_shape,
        in_specs=[spec] * n_in,
        out_specs=[VMEM] * len(out_shape) if many else VMEM,
        scratch_shapes=list(scratch),
        compiler_params=pltpu.CompilerParams(vmem_limit_bytes=limit),
        cost_estimate=pl.CostEstimate(flops=flops, bytes_accessed=1000, transcendentals=0),
    )


def arrived_kernel(*refs):
    total = refs[0][0:8, 0:128]
    for ref in refs[1:-1]:
        total = total + ref[0:8, 0:128]
    refs[-1][...] = total


def round_up(n, m):
    return -(-n // m) * m


class Sizes:
    def __init__(self, tokens, router_t, ids_t, near, layers):
        self.toks, self.width = tokens.shape
        self.experts, self.depth = router_t.shape
        self.topk = ids_t.shape[0]
        self.near, self.layers = near, layers
        self.chips = near // CORES
        self.offsets = list(range(self.chips))
        self.cap = round_up(5 * self.toks * self.topk // (4 * self.experts), 8)
        self.tiles = self.width // self.depth
        self.extra = -(-(1 + self.experts // 8) // self.tiles) * 8
        self.ride = -(-(CORES * self.experts // 8) // self.tiles) * 8

    def tile(self, g):
        r, q = g // self.tiles * 8, g % self.tiles * self.depth
        return slice(r, r + 8), slice(q, q + self.depth)


def pad_kernel(z, tokens_ref, ids_ref, router_ref, out, ids, router, sems):
    copies = [
        pltpu.make_async_copy(tokens_ref, out.at[0 : z.toks, :], sems.at[0]),
        pltpu.make_async_copy(ids_ref, ids, sems.at[1]),
        pltpu.make_async_copy(router_ref, router, sems.at[2]),
    ]
    for copy in copies:
        copy.start()
    out[z.toks : z.toks + z.extra, :] = jnp.zeros((z.extra, z.width), BF16)
    for copy in copies[1:]:
        copy.wait()
    out[z.toks : z.toks + 8, 0 : z.toks] = ids[...].astype(F32).astype(BF16)
    for g in range(z.experts // 8):
        rows, cols = z.tile(g + 1)
        out[z.toks + rows.start : z.toks + rows.stop, cols] = router[8 * g : 8 * g + 8, :]
    copies[0].wait()


def served_expert(z, q):
    return lax.axis_index("expert") * z.near + lax.bitwise_xor(lax.axis_index("zero"), q * CORES)


def ids_of(z, block_ref):
    return block_ref[z.toks : z.toks + 8, 0 : z.toks].astype(F32).astype(jnp.int32)


def slot_marks(z, ids_t):
    has = jnp.concatenate(
        [
            jnp.max((ids_t == served_expert(z, q)).astype(F32), axis=0, keepdims=True)
            for q in z.offsets
        ]
        * 2,
        axis=0,
    )
    earlier = (
        lax.broadcasted_iota(jnp.int32, (z.toks, z.toks), 0)
        < lax.broadcasted_iota(jnp.int32, (z.toks, z.toks), 1)
    ).astype(F32).astype(BF16)
    slot = jnp.dot(has.astype(BF16), earlier, preferred_element_type=F32)
    slot = jnp.where(has > 0, slot, -1.0)
    row = lax.broadcasted_iota(jnp.int32, (z.cap, z.toks), 0).astype(F32)
    return [jnp.where(row == slot[q : q + 1, :], 1.0, 0.0) for q in range(z.chips)]


def pick_kernel(z, n, ride, *refs):
    blocks, outs = refs[:n], refs[n:]
    marks = [jnp.concatenate(slot_marks(z, ids_of(z, b)), axis=0).astype(BF16) for b in blocks]
    part = z.width // PARTS
    for c in range(PARTS):
        cols = slice(c * part, (c + 1) * part)
        rows = [jnp.dot(m, b[0 : z.toks, cols], preferred_element_type=F32) for m, b in zip(marks, blocks)]
        for q in range(z.chips):
            mine = [r[q * z.cap : (q + 1) * z.cap] for r in rows]
            outs[q][0 : n * z.cap, cols] = jnp.concatenate(mine, axis=0).astype(BF16)
    if ride:
        for r in range(CORES):
            for g in range(z.experts // 8):
                rows, cols = z.tile(g + 1)
                piece = blocks[r][z.toks + rows.start : z.toks + rows.stop, cols]
                rows, cols = z.tile(r * (z.experts // 8) + g)
                for q in range(z.chips):
                    outs[q][n * z.cap + rows.start : n * z.cap + rows.stop, cols] = piece


def expert_kernel(z, rows, *refs):
    slabs, gate_ref, up_ref, down_ref = refs[: z.chips], *refs[z.chips : z.chips + 3]
    outs, (x, hidden) = refs[z.chips + 3 : 2 * z.chips + 3], refs[2 * z.chips + 3 :]
    for q in range(z.chips):
        x[q * rows : (q + 1) * rows, :] = slabs[q][0:rows, :]
    ff = gate_ref.shape[1]
    tile = 256
    for f in range(0, ff, tile):
        gate = jnp.dot(x[...], gate_ref[:, f : f + tile], preferred_element_type=F32)
        upper = jnp.dot(x[...], up_ref[:, f : f + tile], preferred_element_type=F32)
        hidden[:, f : f + tile] = (gate / (1.0 + jnp.exp(-gate)) * upper).astype(BF16)
    for c in range(0, z.width, tile):
        y = jnp.dot(hidden[...], down_ref[:, c : c + tile], preferred_element_type=F32)
        for q in range(z.chips):
            outs[q][:, c : c + tile] = y[q * rows : (q + 1) * rows].astype(BF16)


def mix_kernel(z, n, own, *refs):
    blocks, refs = refs[:n], refs[n:]
    if own:
        own_ids, refs = refs[0], refs[1:]
    riders, backs, outs = refs[: z.chips], refs[z.chips : 2 * z.chips], refs[2 * z.chips :]
    number = lax.broadcasted_iota(jnp.int32, (z.experts, z.toks), 0)
    routers = {}
    for i, q in enumerate(z.offsets):
        for r in range(CORES):
            base = CORES * z.cap
            pieces = []
            for g in range(z.experts // 8):
                rows, cols = z.tile(r * (z.experts // 8) + g)
                pieces.append(riders[i][base + rows.start : base + rows.stop, cols].astype(F32))
            routers[CORES * q + r] = jnp.concatenate(pieces, axis=0).astype(BF16)
    for b, block in enumerate(blocks):
        ids_t = own_ids[...] if own and b == 0 else ids_of(z, block)
        logits = None
        for o in range(z.near):
            start = pl.multiple_of(lax.bitwise_xor(lax.axis_index("zero"), o) * z.depth, z.depth)
            term = lax.dot_general(
                routers[o],
                block[0 : z.toks, pl.ds(start, z.depth)],
                (((1,), (1,)), ((), ())),
                preferred_element_type=F32,
            )
            logits = term if logits is None else logits + term
        chosen = number == ids_t[0:1, :]
        for k in range(1, z.topk):
            chosen = chosen | (number == ids_t[k : k + 1, :])
        weights = jnp.where(chosen, jnp.exp(jnp.where(chosen, logits, 0.0)), 0.0)
        gates = weights / jnp.sum(weights, axis=0, keepdims=True)
        marks = slot_marks(z, ids_t)
        mix = []
        for i, q in enumerate(z.offsets):
            gate = jnp.sum(jnp.where(number == served_expert(z, q), gates, 0.0), axis=0, keepdims=True)
            mix.append(marks[i] * gate)
        mix = jnp.concatenate(mix, axis=0).astype(BF16)
        part = z.width // PARTS
        for c in range(PARTS):
            cols = slice(c * part, (c + 1) * part)
            own = slice(b * z.cap, (b + 1) * z.cap)
            y = jnp.concatenate([s[:, cols].astype(F32)[own] for s in backs], axis=0).astype(BF16)
            mixed = lax.dot_general(mix, y, (((0,), (0,)), ((), ())), preferred_element_type=F32).astype(BF16)
            if b == 0:
                outs[0][:, cols] = mixed
            else:
                half = z.toks // 2
                outs[1][:, cols] = mixed[0:half]
                outs[2][:, cols] = mixed[half:]


def join_kernel(*refs):
    out = refs[-1]
    half = out.shape[0] // 2
    for i in range(2):
        rows = slice(i * half, (i + 1) * half)
        total = refs[0][rows, :].astype(F32) + refs[1 + i][...].astype(F32)
        for ref in refs[3:-1]:
            total = total + ref[rows, :].astype(F32)
        out[rows, :] = total.astype(BF16)


def per_device(tokens, router_weight, expert_ids, gate_weight, up_weight, down_weight):
    layers, near = lax.axis_size("expert"), lax.axis_size("zero")
    z = Sizes(tokens, router_weight.T, expert_ids.T, near, layers)

    def along(array, d):
        return lax.ppermute(array, "expert", [(i, (i + d) % layers) for i in range(layers)])

    def across(array, o):
        return lax.ppermute(array, "zero", [(i, i ^ o) for i in range(near)]) if o else array

    def after(arrays, *others):
        return list(lax.optimization_barrier((*arrays, *others))[: len(arrays)])

    def shape(rows):
        return jax.ShapeDtypeStruct((rows, z.width), BF16)

    def pick(blocks, ride, flops=1000):
        n = len(blocks)
        rows = n * z.cap + (z.ride if ride else 0)
        body = functools.partial(pick_kernel, z, n, ride)
        return call(body, [shape(rows)] * z.chips, n, flops=flops)(*blocks)

    def arrived(arrays):
        out = jax.ShapeDtypeStruct((8, 128), BF16)
        return call(arrived_kernel, out, len(arrays), flops=PHASE_FLOPS)(*arrays)

    def slabs_across(slabs):
        return [across(s, CORES * q) for q, s in zip(z.offsets, slabs)]

    def expert(slabs, n, flops=1000):
        rows = n * z.cap
        return call(
            functools.partial(expert_kernel, z, rows),
            [shape(rows)] * z.chips,
            z.chips + 3,
            [
                pltpu.VMEM((z.chips * rows, z.width), BF16),
                pltpu.VMEM((z.chips * rows, gate_weight.shape[2]), BF16),
            ],
            flops,
        )(*slabs, gate_weight[0], up_weight[0], down_weight[0])

    def mix(blocks, backs, own):
        ids = [expert_ids.T] if own else []
        args = [*blocks, *ids, *slots[1], *backs]
        mine, *other = call(
            functools.partial(mix_kernel, z, CORES, own),
            [shape(z.toks), shape(z.toks // 2), shape(z.toks // 2)],
            len(args),
            flops=PHASE_FLOPS,
        )(*args)
        return [mine] + [across(part, 1) for part in other]

    def join(parts):
        return call(join_kernel, shape(z.toks), len(parts))(*parts)

    own = call(
        functools.partial(pad_kernel, z),
        shape(z.toks + z.extra),
        3,
        [
            pltpu.VMEM((z.topk, z.toks), jnp.int32),
            pltpu.VMEM((z.experts, z.depth), BF16),
            pltpu.SemaphoreType.DMA((3,)),
        ],
        spec=pl.BlockSpec(memory_space=pl.ANY),
        limit=PAD_VMEM_LIMIT,
    )(tokens, expert_ids.T, router_weight.T)

    end = layers - 1
    turns = [(d, True) for d in range(end)] + [(d, False) for d in range(1, end)]
    turns += [(end, True), (end, False), (0, False)]
    blocks, pairs, slots, results = {0: own}, {}, {}, {}
    leaving, home, seen, waiting = {}, {}, None, None

    def bring(d):
        if d:
            blocks[d] = after([along(blocks[d - 1], 1)], slots[d - 1][1])[0]
        pairs[d] = [blocks[d], across(blocks[d], 1)]

    for d, outward in turns:
        if outward:
            if d < end:
                bring(d)
            members = after(pairs[d], leaving[d - 2]) if d == end and d > 2 else pairs[d]
            rows = slabs = pick(members, d == 1, PHASE_FLOPS if d == end else 1000)
            if 0 < d < end:
                gate = arrived(slots[d - 1][1:] + ([results[d - 2][0]] if d > 1 else []))
                rows = [after([s], gate)[0] for s in slabs]
                results[d - 1] = expert(after(slots[d - 1], slabs[0]), 2)
            if d == end:
                rows = [after([r], b)[0] for r, b in zip(slabs, seen)]
            seen = slots[d] = slabs_across(rows)
            if d == end - 1:
                bring(end)
                results[d] = expert(after(slots[d], pairs[end][1]), 2)
            if d == end:
                first = [leaving[e] for e in range(1, end)]
                results[d] = expert(after(slots[d], *first), 2, PHASE_FLOPS)
        else:
            rows = [after([r], b)[0] for r, b in zip(results[d], seen)]
            seen = backs = slabs_across(rows)
            first = [(home if d else leaving)[waiting]] if waiting else [results[end - 1][0]]
            members = pairs[d] if d else [tokens, pairs[0][1]]
            sums = mix(members, after(backs, *first), d == 0)
            if d:
                leaving[d] = join(sums)
                home[d] = along(leaving[d], layers - d)
                waiting = d
    return join(sums + [home[d] for d in range(1, layers)])


def solution(mesh):
    everything = ("expert", "zero")
    in_specs = (
        P(everything, None),
        P("zero", None),
        P(everything, None),
        P(everything, None, None),
        P(everything, None, None),
        P(everything, None, None),
    )
    return jax.shard_map(
        per_device, mesh=mesh, in_specs=in_specs, out_specs=P(everything, None), check_vma=False
    )
```

```python
import functools

import jax
import jax.numpy as jnp
from jax import lax
from jax.experimental import pallas as pl
from jax.experimental.pallas import tpu as pltpu
from jax.sharding import PartitionSpec as P

BF16 = jnp.bfloat16
F32 = jnp.float32
VMEM_LIMIT = 32 * 1024 * 1024
PARTS = 4
CORES = 2
PHASE_FLOPS = 50_000_000_000
VMEM = pl.BlockSpec(memory_space=pltpu.VMEM)


def call(body, out_shape, n_in, scratch=(), flops=1000):
    many = isinstance(out_shape, list)
    return pl.pallas_call(
        body,
        out_shape=out_shape,
        in_specs=[VMEM] * n_in,
        out_specs=[VMEM] * len(out_shape) if many else VMEM,
        scratch_shapes=list(scratch),
        compiler_params=pltpu.CompilerParams(vmem_limit_bytes=VMEM_LIMIT),
        cost_estimate=pl.CostEstimate(flops=flops, bytes_accessed=1000, transcendentals=0),
    )


def arrived_kernel(*refs):
    total = refs[0][0:8, 0:128]
    for ref in refs[1:-1]:
        total = total + ref[0:8, 0:128]
    refs[-1][...] = total


def round_up(n, m):
    return -(-n // m) * m


class Sizes:
    def __init__(self, tokens, router_t, ids_t, near, layers):
        self.toks, self.width = tokens.shape
        self.experts, self.depth = router_t.shape
        self.topk = ids_t.shape[0]
        self.near, self.layers = near, layers
        self.chips = near // CORES
        self.cap = round_up(5 * self.toks * self.topk // (4 * self.experts), 8)
        self.tiles = self.width // self.depth
        self.extra = -(-(1 + self.experts // 8) // self.tiles) * 8
        self.ride = -(-(CORES * self.experts // 8) // self.tiles) * 8

    def tile(self, g):
        r, q = g // self.tiles * 8, g % self.tiles * self.depth
        return slice(r, r + 8), slice(q, q + self.depth)


def pad_kernel(z, tokens_ref, ids_ref, router_ref, out):
    out[0 : z.toks, :] = tokens_ref[...]
    blank = jnp.zeros((z.extra, z.width), BF16)
    out[z.toks : z.toks + z.extra, :] = blank
    out[z.toks : z.toks + 8, 0 : z.toks] = ids_ref[...].astype(F32).astype(BF16)
    for g in range(z.experts // 8):
        rows, cols = z.tile(g + 1)
        out[z.toks + rows.start : z.toks + rows.stop, cols] = router_ref[8 * g : 8 * g + 8, :]


def served_expert(z, q):
    return lax.axis_index("expert") * z.near + lax.bitwise_xor(lax.axis_index("zero"), q * CORES)


def ids_of(z, block_ref):
    return block_ref[z.toks : z.toks + 8, 0 : z.toks].astype(F32).astype(jnp.int32)


def slot_marks(z, ids_t, offsets):
    has = jnp.concatenate(
        [
            jnp.max((ids_t == served_expert(z, q)).astype(F32), axis=0, keepdims=True)
            for q in offsets
        ]
        * 2,
        axis=0,
    )
    earlier = (
        lax.broadcasted_iota(jnp.int32, (z.toks, z.toks), 0)
        < lax.broadcasted_iota(jnp.int32, (z.toks, z.toks), 1)
    ).astype(F32).astype(BF16)
    slot = jnp.dot(has.astype(BF16), earlier, preferred_element_type=F32)
    slot = jnp.where(has > 0, slot, -1.0)
    row = lax.broadcasted_iota(jnp.int32, (z.cap, z.toks), 0).astype(F32)
    return [jnp.where(row == slot[q : q + 1, :], 1.0, 0.0) for q in range(z.chips)]


def pick_kernel(z, n, offsets, ride, *refs):
    blocks, outs = refs[:n], refs[n:]
    marks = [jnp.concatenate(slot_marks(z, ids_of(z, b), offsets), axis=0).astype(BF16) for b in blocks]
    part = z.width // PARTS
    for c in range(PARTS):
        cols = slice(c * part, (c + 1) * part)
        rows = [jnp.dot(m, b[0 : z.toks, cols], preferred_element_type=F32) for m, b in zip(marks, blocks)]
        for q in range(z.chips):
            mine = [r[q * z.cap : (q + 1) * z.cap] for r in rows]
            outs[q][0 : n * z.cap, cols] = jnp.concatenate(mine, axis=0).astype(BF16)
    if ride:
        for r in range(CORES):
            for g in range(z.experts // 8):
                rows, cols = z.tile(g + 1)
                piece = blocks[r][z.toks + rows.start : z.toks + rows.stop, cols]
                rows, cols = z.tile(r * (z.experts // 8) + g)
                for q in range(z.chips):
                    outs[q][n * z.cap + rows.start : n * z.cap + rows.stop, cols] = piece


def expert_kernel(z, rows, *refs):
    slabs, gate_ref, up_ref, down_ref = refs[: z.chips], *refs[z.chips : z.chips + 3]
    outs, (x, hidden) = refs[z.chips + 3 : 2 * z.chips + 3], refs[2 * z.chips + 3 :]
    for q in range(z.chips):
        x[q * rows : (q + 1) * rows, :] = slabs[q][0:rows, :]
    ff = gate_ref.shape[1]
    tile = 256
    for f in range(0, ff, tile):
        gate = jnp.dot(x[...], gate_ref[:, f : f + tile], preferred_element_type=F32)
        upper = jnp.dot(x[...], up_ref[:, f : f + tile], preferred_element_type=F32)
        hidden[:, f : f + tile] = (gate / (1.0 + jnp.exp(-gate)) * upper).astype(BF16)
    for c in range(0, z.width, tile):
        y = jnp.dot(hidden[...], down_ref[:, c : c + tile], preferred_element_type=F32)
        for q in range(z.chips):
            outs[q][:, c : c + tile] = y[q * rows : (q + 1) * rows].astype(BF16)


def mix_kernel(z, n, offsets, ride_offsets, *refs):
    blocks, refs = refs[:n], refs[n:]
    riders, backs, outs = refs[: z.chips], refs[z.chips : 2 * z.chips], refs[2 * z.chips :]
    number = lax.broadcasted_iota(jnp.int32, (z.experts, z.toks), 0)
    routers = {}
    for i, q in enumerate(ride_offsets):
        for r in range(CORES):
            base = CORES * z.cap
            pieces = []
            for g in range(z.experts // 8):
                rows, cols = z.tile(r * (z.experts // 8) + g)
                pieces.append(riders[i][base + rows.start : base + rows.stop, cols].astype(F32))
            routers[CORES * q + r] = jnp.concatenate(pieces, axis=0).astype(BF16)
    for b, block in enumerate(blocks):
        ids_t = ids_of(z, block)
        logits = None
        for o in range(z.near):
            start = pl.multiple_of(lax.bitwise_xor(lax.axis_index("zero"), o) * z.depth, z.depth)
            term = lax.dot_general(
                routers[o],
                block[0 : z.toks, pl.ds(start, z.depth)],
                (((1,), (1,)), ((), ())),
                preferred_element_type=F32,
            )
            logits = term if logits is None else logits + term
        chosen = number == ids_t[0:1, :]
        for k in range(1, z.topk):
            chosen = chosen | (number == ids_t[k : k + 1, :])
        weights = jnp.where(chosen, jnp.exp(jnp.where(chosen, logits, 0.0)), 0.0)
        gates = weights / jnp.sum(weights, axis=0, keepdims=True)
        marks = slot_marks(z, ids_t, offsets)
        mix = []
        for mark, q in zip(marks, offsets):
            gate = jnp.sum(jnp.where(number == served_expert(z, q), gates, 0.0), axis=0, keepdims=True)
            mix.append(mark * gate)
        mix = jnp.concatenate(mix, axis=0).astype(BF16)
        part = z.width // PARTS
        for c in range(PARTS):
            cols = slice(c * part, (c + 1) * part)
            own = slice(b * z.cap, (b + 1) * z.cap)
            y = jnp.concatenate([s[:, cols].astype(F32)[own] for s in backs], axis=0).astype(BF16)
            mixed = lax.dot_general(mix, y, (((0,), (0,)), ((), ())), preferred_element_type=F32).astype(BF16)
            if b == 0:
                outs[0][:, cols] = mixed
            else:
                half = z.toks // 2
                outs[1][:, cols] = mixed[0:half]
                outs[2][:, cols] = mixed[half:]


def join_kernel(*refs):
    out = refs[-1]
    half = out.shape[0] // 2
    for i in range(2):
        rows = slice(i * half, (i + 1) * half)
        total = refs[0][rows, :].astype(F32) + refs[1 + i][...].astype(F32)
        for ref in refs[3:-1]:
            total = total + ref[rows, :].astype(F32)
        out[rows, :] = total.astype(BF16)


def per_device(tokens, router_weight, expert_ids, gate_weight, up_weight, down_weight):
    layers, near = lax.axis_size("expert"), lax.axis_size("zero")
    z = Sizes(tokens, router_weight.T, expert_ids.T, near, layers)

    def along(array, d):
        return lax.ppermute(array, "expert", [(i, (i + d) % layers) for i in range(layers)])

    def across(array, o):
        return lax.ppermute(array, "zero", [(i, i ^ o) for i in range(near)]) if o else array

    def after(arrays, *others):
        return list(lax.optimization_barrier((*arrays, *others))[: len(arrays)])

    def shape(rows):
        return jax.ShapeDtypeStruct((rows, z.width), BF16)

    forward = list(range(z.chips))
    backward = [0] + forward[:0:-1]
    out_order = {0: forward, 1: forward[:-2] + forward[:-3:-1]}
    ride_order = out_order[1]

    def pick(blocks, d, flops=1000):
        n = len(blocks)
        offsets = out_order.get(d, backward)
        rows = n * z.cap + (z.ride if d == 1 else 0)
        body = functools.partial(pick_kernel, z, n, offsets, d == 1)
        return dict(zip(offsets, call(body, [shape(rows)] * z.chips, n, flops=flops)(*blocks)))

    def arrived(arrays):
        out = jax.ShapeDtypeStruct((8, 128), BF16)
        return call(arrived_kernel, out, len(arrays), flops=PHASE_FLOPS)(*arrays)

    def slabs_across(slabs):
        return {q: across(s, CORES * q) for q, s in slabs.items()}

    def expert(slabs, *first, flops=1000):
        rows = CORES * z.cap
        offsets = list(slabs)
        outs = call(
            functools.partial(expert_kernel, z, rows),
            [shape(rows)] * z.chips,
            z.chips + 3,
            [
                pltpu.VMEM((z.chips * rows, z.width), BF16),
                pltpu.VMEM((z.chips * rows, gate_weight.shape[2]), BF16),
            ],
            flops,
        )(*after(list(slabs.values()), *first), gate_weight[0], up_weight[0], down_weight[0])
        return dict(zip(offsets, outs))

    def mix(blocks, backs, *first):
        riders = [slots[1][q] for q in ride_order]
        n = len(blocks)
        mine, *other = call(
            functools.partial(mix_kernel, z, n, list(backs), ride_order),
            [shape(z.toks), shape(z.toks // 2), shape(z.toks // 2)],
            n + 2 * z.chips,
            flops=PHASE_FLOPS,
        )(*blocks, *riders, *after(list(backs.values()), *first))
        return [mine] + [across(part, 1) for part in other]

    def join(parts):
        return call(join_kernel, shape(z.toks), len(parts))(*parts)

    own = call(functools.partial(pad_kernel, z), shape(z.toks + z.extra), 3)(
        tokens, expert_ids.T, router_weight.T
    )

    end = layers - 1
    turns = [(d, True) for d in range(end)] + [(d, False) for d in range(1, end)]
    turns += [(end, True), (end, False), (0, False)]
    blocks, pairs, slots, results = {0: own}, {}, {}, {}
    leaving, home, seen, waiting = {}, {}, None, None
    for d, outward in turns:
        if outward:
            if d:
                blocks[d] = after([along(blocks[d - 1], 1)], slots[d - 1][1])[0]
            pairs[d] = [blocks[d], across(blocks[d], 1)]
            rows = slabs = pick(pairs[d], d, PHASE_FLOPS if d == end else 1000)
            if 0 < d < end:
                gate = [slots[d - 1][q] for q in forward[1:]] + ([results[d - 2][0]] if d > 1 else [])
                gate = arrived(gate)
                rows = {q: after([s], gate)[0] for q, s in slabs.items()}
                results[d - 1] = expert(slots[d - 1], slabs[0])
            if d == end:
                rows = {q: after([s], seen[q])[0] for q, s in slabs.items()}
            seen = slots[d] = slabs_across(rows)
            if d == end - 1:
                results[d] = expert(slots[d])
            if d == end:
                first = [leaving[e] for e in range(1, end)]
                results[d] = expert(slots[d], *first, flops=PHASE_FLOPS)
        else:
            rows = {q: after([results[d][q]], seen[q])[0] for q in backward}
            seen = backs = slabs_across(rows)
            first = [(home if d else leaving)[waiting]] if waiting else [results[end - 1][0]]
            sums = mix(pairs[d], backs, *first)
            if d:
                leaving[d] = join(sums)
                home[d] = along(leaving[d], layers - d)
                waiting = d
    return join(sums + [home[d] for d in range(1, layers)])


def solution(mesh):
    everything = ("expert", "zero")
    in_specs = (
        P(everything, None),
        P("zero", None),
        P(everything, None),
        P(everything, None, None),
        P(everything, None, None),
        P(everything, None, None),
    )
    return jax.shard_map(
        per_device, mesh=mesh, in_specs=in_specs, out_specs=P(everything, None), check_vma=False
    )
```

```python
import functools

import jax
import jax.numpy as jnp
from jax import lax
from jax.experimental import pallas as pl
from jax.experimental.pallas import tpu as pltpu
from jax.sharding import PartitionSpec as P

BF16 = jnp.bfloat16
F32 = jnp.float32
VMEM_LIMIT = 32 * 1024 * 1024
PARTS = 4
CORES = 2
PHASE_FLOPS = 20_000_000_000
VMEM = pl.BlockSpec(memory_space=pltpu.VMEM)


def call(body, out_shape, n_in, scratch=(), flops=1000):
    many = isinstance(out_shape, list)
    return pl.pallas_call(
        body,
        out_shape=out_shape,
        in_specs=[VMEM] * n_in,
        out_specs=[VMEM] * len(out_shape) if many else VMEM,
        scratch_shapes=list(scratch),
        compiler_params=pltpu.CompilerParams(vmem_limit_bytes=VMEM_LIMIT),
        cost_estimate=pl.CostEstimate(flops=flops, bytes_accessed=1000, transcendentals=0),
    )


def arrived_kernel(*refs):
    total = refs[0][0:8, 0:128]
    for ref in refs[1:-1]:
        total = total + ref[0:8, 0:128]
    refs[-1][...] = total


def round_up(n, m):
    return -(-n // m) * m


class Sizes:
    def __init__(self, tokens, router_t, ids_t, near, layers):
        self.toks, self.width = tokens.shape
        self.experts, self.depth = router_t.shape
        self.topk = ids_t.shape[0]
        self.near, self.layers = near, layers
        self.chips = near // CORES
        self.cap = round_up(5 * self.toks * self.topk // (4 * self.experts), 8)
        self.tiles = self.width // self.depth
        self.extra = -(-(1 + self.experts // 8) // self.tiles) * 8
        self.ride = -(-(CORES * self.experts // 8) // self.tiles) * 8

    def tile(self, g):
        r, q = g // self.tiles * 8, g % self.tiles * self.depth
        return slice(r, r + 8), slice(q, q + self.depth)


def pad_kernel(z, tokens_ref, ids_ref, router_ref, out):
    out[0 : z.toks, :] = tokens_ref[...]
    blank = jnp.zeros((z.extra, z.width), BF16)
    out[z.toks : z.toks + z.extra, :] = blank
    out[z.toks : z.toks + 8, 0 : z.toks] = ids_ref[...].astype(F32).astype(BF16)
    for g in range(z.experts // 8):
        rows, cols = z.tile(g + 1)
        out[z.toks + rows.start : z.toks + rows.stop, cols] = router_ref[8 * g : 8 * g + 8, :]


def served_expert(z, q):
    return lax.axis_index("expert") * z.near + lax.bitwise_xor(lax.axis_index("zero"), q * CORES)


def ids_of(z, block_ref):
    return block_ref[z.toks : z.toks + 8, 0 : z.toks].astype(F32).astype(jnp.int32)


def slot_marks(z, ids_t, offsets):
    has = jnp.concatenate(
        [
            jnp.max((ids_t == served_expert(z, q)).astype(F32), axis=0, keepdims=True)
            for q in offsets
        ]
        * 2,
        axis=0,
    )
    earlier = (
        lax.broadcasted_iota(jnp.int32, (z.toks, z.toks), 0)
        < lax.broadcasted_iota(jnp.int32, (z.toks, z.toks), 1)
    ).astype(F32).astype(BF16)
    slot = jnp.dot(has.astype(BF16), earlier, preferred_element_type=F32)
    slot = jnp.where(has > 0, slot, -1.0)
    row = lax.broadcasted_iota(jnp.int32, (z.cap, z.toks), 0).astype(F32)
    return [jnp.where(row == slot[q : q + 1, :], 1.0, 0.0) for q in range(z.chips)]


def pick_kernel(z, n, offsets, ride, *refs):
    blocks, outs = refs[:n], refs[n:]
    marks = [jnp.concatenate(slot_marks(z, ids_of(z, b), offsets), axis=0).astype(BF16) for b in blocks]
    part = z.width // PARTS
    for c in range(PARTS):
        cols = slice(c * part, (c + 1) * part)
        rows = [jnp.dot(m, b[0 : z.toks, cols], preferred_element_type=F32) for m, b in zip(marks, blocks)]
        for q in range(z.chips):
            mine = [r[q * z.cap : (q + 1) * z.cap] for r in rows]
            outs[q][0 : n * z.cap, cols] = jnp.concatenate(mine, axis=0).astype(BF16)
    if ride:
        for r in range(CORES):
            for g in range(z.experts // 8):
                rows, cols = z.tile(g + 1)
                piece = blocks[r][z.toks + rows.start : z.toks + rows.stop, cols]
                rows, cols = z.tile(r * (z.experts // 8) + g)
                for q in range(z.chips):
                    outs[q][n * z.cap + rows.start : n * z.cap + rows.stop, cols] = piece


def expert_kernel(z, rows, *refs):
    slabs, gate_ref, up_ref, down_ref = refs[: z.chips], *refs[z.chips : z.chips + 3]
    outs, (x, hidden) = refs[z.chips + 3 : 2 * z.chips + 3], refs[2 * z.chips + 3 :]
    for q in range(z.chips):
        x[q * rows : (q + 1) * rows, :] = slabs[q][0:rows, :]
    ff = gate_ref.shape[1]
    tile = 256
    for f in range(0, ff, tile):
        gate = jnp.dot(x[...], gate_ref[:, f : f + tile], preferred_element_type=F32)
        upper = jnp.dot(x[...], up_ref[:, f : f + tile], preferred_element_type=F32)
        hidden[:, f : f + tile] = (gate / (1.0 + jnp.exp(-gate)) * upper).astype(BF16)
    for c in range(0, z.width, tile):
        y = jnp.dot(hidden[...], down_ref[:, c : c + tile], preferred_element_type=F32)
        for q in range(z.chips):
            outs[q][:, c : c + tile] = y[q * rows : (q + 1) * rows].astype(BF16)


def mix_kernel(z, n, offsets, ride_offsets, *refs):
    blocks, refs = refs[:n], refs[n:]
    riders, backs, outs = refs[: z.chips], refs[z.chips : 2 * z.chips], refs[2 * z.chips :]
    number = lax.broadcasted_iota(jnp.int32, (z.experts, z.toks), 0)
    routers = {}
    for i, q in enumerate(ride_offsets):
        for r in range(CORES):
            base = CORES * z.cap
            pieces = []
            for g in range(z.experts // 8):
                rows, cols = z.tile(r * (z.experts // 8) + g)
                pieces.append(riders[i][base + rows.start : base + rows.stop, cols].astype(F32))
            routers[CORES * q + r] = jnp.concatenate(pieces, axis=0).astype(BF16)
    for b, block in enumerate(blocks):
        ids_t = ids_of(z, block)
        logits = None
        for o in range(z.near):
            start = pl.multiple_of(lax.bitwise_xor(lax.axis_index("zero"), o) * z.depth, z.depth)
            term = lax.dot_general(
                routers[o],
                block[0 : z.toks, pl.ds(start, z.depth)],
                (((1,), (1,)), ((), ())),
                preferred_element_type=F32,
            )
            logits = term if logits is None else logits + term
        chosen = number == ids_t[0:1, :]
        for k in range(1, z.topk):
            chosen = chosen | (number == ids_t[k : k + 1, :])
        weights = jnp.where(chosen, jnp.exp(jnp.where(chosen, logits, 0.0)), 0.0)
        gates = weights / jnp.sum(weights, axis=0, keepdims=True)
        marks = slot_marks(z, ids_t, offsets)
        mix = []
        for mark, q in zip(marks, offsets):
            gate = jnp.sum(jnp.where(number == served_expert(z, q), gates, 0.0), axis=0, keepdims=True)
            mix.append(mark * gate)
        mix = jnp.concatenate(mix, axis=0).astype(BF16)
        part = z.width // PARTS
        for c in range(PARTS):
            cols = slice(c * part, (c + 1) * part)
            own = slice(b * z.cap, (b + 1) * z.cap)
            y = jnp.concatenate([s[:, cols].astype(F32)[own] for s in backs], axis=0).astype(BF16)
            mixed = lax.dot_general(mix, y, (((0,), (0,)), ((), ())), preferred_element_type=F32).astype(BF16)
            if b == 0:
                outs[0][:, cols] = mixed
            else:
                half = z.toks // 2
                outs[1][:, cols] = mixed[0:half]
                outs[2][:, cols] = mixed[half:]


def join_kernel(*refs):
    out = refs[-1]
    half = out.shape[0] // 2
    for i in range(2):
        rows = slice(i * half, (i + 1) * half)
        total = refs[0][rows, :].astype(F32) + refs[1 + i][...].astype(F32)
        for ref in refs[3:-1]:
            total = total + ref[rows, :].astype(F32)
        out[rows, :] = total.astype(BF16)


def per_device(tokens, router_weight, expert_ids, gate_weight, up_weight, down_weight):
    layers, near = lax.axis_size("expert"), lax.axis_size("zero")
    z = Sizes(tokens, router_weight.T, expert_ids.T, near, layers)

    def along(array, d):
        return lax.ppermute(array, "expert", [(i, (i + d) % layers) for i in range(layers)])

    def across(array, o):
        return lax.ppermute(array, "zero", [(i, i ^ o) for i in range(near)]) if o else array

    def after(arrays, *others):
        return list(lax.optimization_barrier((*arrays, *others))[: len(arrays)])

    def shape(rows):
        return jax.ShapeDtypeStruct((rows, z.width), BF16)

    forward = list(range(z.chips))
    backward = [0] + forward[:0:-1]
    out_order = {0: forward, 1: forward[:-2] + forward[:-3:-1]}
    ride_order = out_order[1]

    def pick(blocks, d, flops=1000):
        n = len(blocks)
        offsets = out_order.get(d, backward)
        rows = n * z.cap + (z.ride if d == 1 else 0)
        body = functools.partial(pick_kernel, z, n, offsets, d == 1)
        return dict(zip(offsets, call(body, [shape(rows)] * z.chips, n, flops=flops)(*blocks)))

    def arrived(arrays):
        out = jax.ShapeDtypeStruct((8, 128), BF16)
        return call(arrived_kernel, out, len(arrays), flops=PHASE_FLOPS)(*arrays)

    def slabs_across(slabs):
        return {q: across(s, CORES * q) for q, s in slabs.items()}

    def expert(slabs, *first, flops=1000):
        rows = CORES * z.cap
        offsets = list(slabs)
        outs = call(
            functools.partial(expert_kernel, z, rows),
            [shape(rows)] * z.chips,
            z.chips + 3,
            [
                pltpu.VMEM((z.chips * rows, z.width), BF16),
                pltpu.VMEM((z.chips * rows, gate_weight.shape[2]), BF16),
            ],
            flops,
        )(*after(list(slabs.values()), *first), gate_weight[0], up_weight[0], down_weight[0])
        return dict(zip(offsets, outs))

    def mix(blocks, backs, *first):
        riders = [slots[1][q] for q in ride_order]
        n = len(blocks)
        mine, *other = call(
            functools.partial(mix_kernel, z, n, list(backs), ride_order),
            [shape(z.toks), shape(z.toks // 2), shape(z.toks // 2)],
            n + 2 * z.chips,
            flops=PHASE_FLOPS,
        )(*blocks, *riders, *after(list(backs.values()), *first))
        return [mine] + [across(part, 1) for part in other]

    def join(parts):
        return call(join_kernel, shape(z.toks), len(parts))(*parts)

    own = call(functools.partial(pad_kernel, z), shape(z.toks + z.extra), 3)(
        tokens, expert_ids.T, router_weight.T
    )

    end = layers - 1
    turns = [(d, True) for d in range(end)] + [(d, False) for d in range(1, end)]
    turns += [(end, True), (end, False), (0, False)]
    blocks, pairs, slots, results = {0: own}, {}, {}, {}
    leaving, home, seen, waiting = {}, {}, None, None
    for d, outward in turns:
        if outward:
            if d:
                blocks[d] = after([along(blocks[d - 1], 1)], slots[d - 1][1])[0]
            pairs[d] = [blocks[d], across(blocks[d], 1)]
            rows = slabs = pick(pairs[d], d, PHASE_FLOPS if d == end else 1000)
            if 0 < d < end:
                gate = [slots[d - 1][q] for q in forward[1:]] + ([results[d - 2][0]] if d > 1 else [])
                gate = arrived(gate)
                rows = {q: after([s], gate)[0] for q, s in slabs.items()}
                results[d - 1] = expert(slots[d - 1], slabs[0])
            if d == end:
                rows = {q: after([s], seen[q])[0] for q, s in slabs.items()}
            seen = slots[d] = slabs_across(rows)
            if d == end - 1:
                results[d] = expert(slots[d])
            if d == end:
                first = [leaving[e] for e in range(1, end)]
                results[d] = expert(slots[d], *first, flops=PHASE_FLOPS)
        else:
            rows = {q: after([results[d][q]], seen[q])[0] for q in backward}
            seen = backs = slabs_across(rows)
            first = [(home if d else leaving)[waiting]] if waiting else [results[end - 1][0]]
            sums = mix(pairs[d], backs, *first)
            if d:
                leaving[d] = join(sums)
                home[d] = along(leaving[d], layers - d)
                waiting = d
    return join(sums + [home[d] for d in range(1, layers)])


def solution(mesh):
    everything = ("expert", "zero")
    in_specs = (
        P(everything, None),
        P("zero", None),
        P(everything, None),
        P(everything, None, None),
        P(everything, None, None),
        P(everything, None, None),
    )
    return jax.shard_map(
        per_device, mesh=mesh, in_specs=in_specs, out_specs=P(everything, None), check_vma=False
    )
```

```python
import functools

import jax
import jax.numpy as jnp
from jax import lax
from jax.experimental import pallas as pl
from jax.experimental.pallas import tpu as pltpu
from jax.sharding import PartitionSpec as P

BF16 = jnp.bfloat16
F32 = jnp.float32
VMEM_LIMIT = 32 * 1024 * 1024
PARTS = 4
CORES = 2
PHASE_FLOPS = 20_000_000_000
VMEM = pl.BlockSpec(memory_space=pltpu.VMEM)


def call(body, out_shape, n_in, scratch=(), flops=1000):
    many = isinstance(out_shape, list)
    return pl.pallas_call(
        body,
        out_shape=out_shape,
        in_specs=[VMEM] * n_in,
        out_specs=[VMEM] * len(out_shape) if many else VMEM,
        scratch_shapes=list(scratch),
        compiler_params=pltpu.CompilerParams(vmem_limit_bytes=VMEM_LIMIT),
        cost_estimate=pl.CostEstimate(flops=flops, bytes_accessed=1000, transcendentals=0),
    )


def arrived_kernel(*refs):
    total = refs[0][0:8, 0:128]
    for ref in refs[1:-1]:
        total = total + ref[0:8, 0:128]
    refs[-1][...] = total


def round_up(n, m):
    return -(-n // m) * m


class Sizes:
    def __init__(self, tokens, router_t, ids_t, near, layers):
        self.toks, self.width = tokens.shape
        self.experts, self.depth = router_t.shape
        self.topk = ids_t.shape[0]
        self.near, self.layers = near, layers
        self.chips = near // CORES
        self.cap = round_up(5 * self.toks * self.topk // (4 * self.experts), 8)
        self.tiles = self.width // self.depth
        self.extra = -(-(1 + self.experts // 8) // self.tiles) * 8
        self.ride = -(-(CORES * self.experts // 8) // self.tiles) * 8

    def tile(self, g):
        r, q = g // self.tiles * 8, g % self.tiles * self.depth
        return slice(r, r + 8), slice(q, q + self.depth)


def pad_kernel(z, tokens_ref, ids_ref, router_ref, out):
    out[0 : z.toks, :] = tokens_ref[...]
    blank = jnp.zeros((z.extra, z.width), BF16)
    out[z.toks : z.toks + z.extra, :] = blank
    out[z.toks : z.toks + 8, 0 : z.toks] = ids_ref[...].astype(F32).astype(BF16)
    for g in range(z.experts // 8):
        rows, cols = z.tile(g + 1)
        out[z.toks + rows.start : z.toks + rows.stop, cols] = router_ref[8 * g : 8 * g + 8, :]


def served_expert(z, q):
    return lax.axis_index("expert") * z.near + lax.bitwise_xor(lax.axis_index("zero"), q * CORES)


def ids_of(z, block_ref):
    return block_ref[z.toks : z.toks + 8, 0 : z.toks].astype(F32).astype(jnp.int32)


def slot_marks(z, ids_t, offsets):
    has = jnp.concatenate(
        [
            jnp.max((ids_t == served_expert(z, q)).astype(F32), axis=0, keepdims=True)
            for q in offsets
        ]
        * 2,
        axis=0,
    )
    earlier = (
        lax.broadcasted_iota(jnp.int32, (z.toks, z.toks), 0)
        < lax.broadcasted_iota(jnp.int32, (z.toks, z.toks), 1)
    ).astype(F32).astype(BF16)
    slot = jnp.dot(has.astype(BF16), earlier, preferred_element_type=F32)
    slot = jnp.where(has > 0, slot, -1.0)
    row = lax.broadcasted_iota(jnp.int32, (z.cap, z.toks), 0).astype(F32)
    return [jnp.where(row == slot[q : q + 1, :], 1.0, 0.0) for q in range(z.chips)]


def pick_kernel(z, n, offsets, ride, *refs):
    blocks, outs = refs[:n], refs[n:]
    marks = [jnp.concatenate(slot_marks(z, ids_of(z, b), offsets), axis=0).astype(BF16) for b in blocks]
    part = z.width // PARTS
    for c in range(PARTS):
        cols = slice(c * part, (c + 1) * part)
        rows = [jnp.dot(m, b[0 : z.toks, cols], preferred_element_type=F32) for m, b in zip(marks, blocks)]
        for q in range(z.chips):
            mine = [r[q * z.cap : (q + 1) * z.cap] for r in rows]
            outs[q][0 : n * z.cap, cols] = jnp.concatenate(mine, axis=0).astype(BF16)
    if ride:
        for r in range(CORES):
            for g in range(z.experts // 8):
                rows, cols = z.tile(g + 1)
                piece = blocks[r][z.toks + rows.start : z.toks + rows.stop, cols]
                rows, cols = z.tile(r * (z.experts // 8) + g)
                for q in range(z.chips):
                    outs[q][n * z.cap + rows.start : n * z.cap + rows.stop, cols] = piece


def expert_kernel(z, rows, *refs):
    slabs, gate_ref, up_ref, down_ref = refs[: z.chips], *refs[z.chips : z.chips + 3]
    outs, (x, hidden) = refs[z.chips + 3 : 2 * z.chips + 3], refs[2 * z.chips + 3 :]
    for q in range(z.chips):
        x[q * rows : (q + 1) * rows, :] = slabs[q][0:rows, :]
    ff = gate_ref.shape[1]
    tile = 256
    for f in range(0, ff, tile):
        gate = jnp.dot(x[...], gate_ref[:, f : f + tile], preferred_element_type=F32)
        upper = jnp.dot(x[...], up_ref[:, f : f + tile], preferred_element_type=F32)
        hidden[:, f : f + tile] = (gate / (1.0 + jnp.exp(-gate)) * upper).astype(BF16)
    for c in range(0, z.width, tile):
        y = jnp.dot(hidden[...], down_ref[:, c : c + tile], preferred_element_type=F32)
        for q in range(z.chips):
            outs[q][:, c : c + tile] = y[q * rows : (q + 1) * rows].astype(BF16)


def mix_kernel(z, n, offsets, ride_offsets, *refs):
    blocks, refs = refs[:n], refs[n:]
    riders, backs, outs = refs[: z.chips], refs[z.chips : 2 * z.chips], refs[2 * z.chips :]
    number = lax.broadcasted_iota(jnp.int32, (z.experts, z.toks), 0)
    routers = {}
    for i, q in enumerate(ride_offsets):
        for r in range(CORES):
            base = CORES * z.cap
            pieces = []
            for g in range(z.experts // 8):
                rows, cols = z.tile(r * (z.experts // 8) + g)
                pieces.append(riders[i][base + rows.start : base + rows.stop, cols].astype(F32))
            routers[CORES * q + r] = jnp.concatenate(pieces, axis=0).astype(BF16)
    for b, block in enumerate(blocks):
        ids_t = ids_of(z, block)
        logits = None
        for o in range(z.near):
            start = pl.multiple_of(lax.bitwise_xor(lax.axis_index("zero"), o) * z.depth, z.depth)
            term = lax.dot_general(
                routers[o],
                block[0 : z.toks, pl.ds(start, z.depth)],
                (((1,), (1,)), ((), ())),
                preferred_element_type=F32,
            )
            logits = term if logits is None else logits + term
        chosen = number == ids_t[0:1, :]
        for k in range(1, z.topk):
            chosen = chosen | (number == ids_t[k : k + 1, :])
        weights = jnp.where(chosen, jnp.exp(jnp.where(chosen, logits, 0.0)), 0.0)
        gates = weights / jnp.sum(weights, axis=0, keepdims=True)
        marks = slot_marks(z, ids_t, offsets)
        mix = []
        for mark, q in zip(marks, offsets):
            gate = jnp.sum(jnp.where(number == served_expert(z, q), gates, 0.0), axis=0, keepdims=True)
            mix.append(mark * gate)
        mix = jnp.concatenate(mix, axis=0).astype(BF16)
        part = z.width // PARTS
        for c in range(PARTS):
            cols = slice(c * part, (c + 1) * part)
            own = slice(b * z.cap, (b + 1) * z.cap)
            y = jnp.concatenate([s[:, cols].astype(F32)[own] for s in backs], axis=0).astype(BF16)
            mixed = lax.dot_general(mix, y, (((0,), (0,)), ((), ())), preferred_element_type=F32).astype(BF16)
            if b == 0:
                outs[0][:, cols] = mixed
            else:
                half = z.toks // 2
                outs[1][:, cols] = mixed[0:half]
                outs[2][:, cols] = mixed[half:]


def join_kernel(*refs):
    out = refs[-1]
    half = out.shape[0] // 2
    for i in range(2):
        rows = slice(i * half, (i + 1) * half)
        total = refs[0][rows, :].astype(F32) + refs[1 + i][...].astype(F32)
        for ref in refs[3:-1]:
            total = total + ref[rows, :].astype(F32)
        out[rows, :] = total.astype(BF16)


def per_device(tokens, router_weight, expert_ids, gate_weight, up_weight, down_weight):
    layers, near = lax.axis_size("expert"), lax.axis_size("zero")
    z = Sizes(tokens, router_weight.T, expert_ids.T, near, layers)

    def along(array, d):
        return lax.ppermute(array, "expert", [(i, (i + d) % layers) for i in range(layers)])

    def across(array, o):
        return lax.ppermute(array, "zero", [(i, i ^ o) for i in range(near)]) if o else array

    def after(arrays, *others):
        return list(lax.optimization_barrier((*arrays, *others))[: len(arrays)])

    def shape(rows):
        return jax.ShapeDtypeStruct((rows, z.width), BF16)

    forward = list(range(z.chips))
    backward = [0] + forward[:0:-1]
    out_order = {0: forward, 1: forward[:-2] + forward[:-3:-1]}
    ride_order = out_order[1]

    def pick(blocks, d, flops=1000):
        n = len(blocks)
        offsets = out_order.get(d, backward)
        rows = n * z.cap + (z.ride if d == 1 else 0)
        body = functools.partial(pick_kernel, z, n, offsets, d == 1)
        return dict(zip(offsets, call(body, [shape(rows)] * z.chips, n, flops=flops)(*blocks)))

    def arrived(arrays):
        out = jax.ShapeDtypeStruct((8, 128), BF16)
        return call(arrived_kernel, out, len(arrays), flops=PHASE_FLOPS)(*arrays)

    def slabs_across(slabs):
        return {q: across(s, CORES * q) for q, s in slabs.items()}

    def expert(slabs, *first, flops=1000):
        rows = CORES * z.cap
        offsets = list(slabs)
        outs = call(
            functools.partial(expert_kernel, z, rows),
            [shape(rows)] * z.chips,
            z.chips + 3,
            [
                pltpu.VMEM((z.chips * rows, z.width), BF16),
                pltpu.VMEM((z.chips * rows, gate_weight.shape[2]), BF16),
            ],
            flops,
        )(*after(list(slabs.values()), *first), gate_weight[0], up_weight[0], down_weight[0])
        return dict(zip(offsets, outs))

    def mix(blocks, backs, *first):
        riders = [slots[1][q] for q in ride_order]
        n = len(blocks)
        mine, *other = call(
            functools.partial(mix_kernel, z, n, list(backs), ride_order),
            [shape(z.toks), shape(z.toks // 2), shape(z.toks // 2)],
            n + 2 * z.chips,
            flops=PHASE_FLOPS,
        )(*blocks, *riders, *after(list(backs.values()), *first))
        return [mine] + [across(part, 1) for part in other]

    def join(parts):
        return call(join_kernel, shape(z.toks), len(parts))(*parts)

    own = call(functools.partial(pad_kernel, z), shape(z.toks + z.extra), 3)(
        tokens, expert_ids.T, router_weight.T
    )

    end = layers - 1
    turns = [(d, True) for d in range(end)] + [(d, False) for d in range(1, end)]
    turns += [(end, True), (end, False), (0, False)]
    blocks, pairs, slots, results = {0: own}, {}, {}, {}
    leaving, home, seen, waiting = {}, {}, None, None
    for d, outward in turns:
        if outward:
            if d:
                blocks[d] = after([along(blocks[d - 1], 1)], slots[d - 1][1])[0]
            pairs[d] = [blocks[d], across(blocks[d], 1)]
            rows = slabs = pick(pairs[d], d, PHASE_FLOPS if d == end else 1000)
            if 0 < d < end:
                gate = [slots[d - 1][q] for q in forward[1:]] + ([results[d - 2][0]] if d > 1 else [])
                gate = arrived(gate)
                rows = {q: after([s], gate)[0] for q, s in slabs.items()}
                results[d - 1] = expert(slots[d - 1], slabs[0])
            if d == end:
                rows = {q: after([s], seen[q])[0] for q, s in slabs.items()}
            seen = slots[d] = slabs_across(rows)
            if d == end - 1:
                results[d] = expert(slots[d])
            if d == end:
                first = [leaving[e] for e in range(1, end)]
                results[d] = expert(slots[d], *first, flops=PHASE_FLOPS)
        else:
            rows = {q: after([results[d][q]], seen[q])[0] for q in backward}
            if d == 0:
                rows[forward[-1]] = after([rows[forward[-1]]], sums[0])[0]
            seen = backs = slabs_across(rows)
            first = [(home if d else leaving)[waiting]] if waiting else [results[end - 1][0]]
            sums = mix(pairs[d], backs, *first)
            if d:
                leaving[d] = join(sums)
                home[d] = along(leaving[d], layers - d)
                waiting = d
    return join(sums + [home[d] for d in range(1, layers)])


def solution(mesh):
    everything = ("expert", "zero")
    in_specs = (
        P(everything, None),
        P("zero", None),
        P(everything, None),
        P(everything, None, None),
        P(everything, None, None),
        P(everything, None, None),
    )
    return jax.shard_map(
        per_device, mesh=mesh, in_specs=in_specs, out_specs=P(everything, None), check_vma=False
    )
```

```python
import functools

import jax
import jax.numpy as jnp
from jax import lax
from jax.experimental import pallas as pl
from jax.experimental.pallas import tpu as pltpu
from jax.sharding import PartitionSpec as P

BF16 = jnp.bfloat16
F32 = jnp.float32
VMEM_LIMIT = 32 * 1024 * 1024
PARTS = 4
CORES = 2
PHASE_FLOPS = 20_000_000_000
VMEM = pl.BlockSpec(memory_space=pltpu.VMEM)


def call(body, out_shape, n_in, scratch=(), flops=1000):
    many = isinstance(out_shape, list)
    return pl.pallas_call(
        body,
        out_shape=out_shape,
        in_specs=[VMEM] * n_in,
        out_specs=[VMEM] * len(out_shape) if many else VMEM,
        scratch_shapes=list(scratch),
        compiler_params=pltpu.CompilerParams(vmem_limit_bytes=VMEM_LIMIT),
        cost_estimate=pl.CostEstimate(flops=flops, bytes_accessed=1000, transcendentals=0),
    )


def arrived_kernel(*refs):
    total = refs[0][0:8, 0:128]
    for ref in refs[1:-1]:
        total = total + ref[0:8, 0:128]
    refs[-1][...] = total


def round_up(n, m):
    return -(-n // m) * m


class Sizes:
    def __init__(self, tokens, router_t, ids_t, near, layers):
        self.toks, self.width = tokens.shape
        self.experts, self.depth = router_t.shape
        self.topk = ids_t.shape[0]
        self.near, self.layers = near, layers
        self.chips = near // CORES
        self.cap = round_up(5 * self.toks * self.topk // (4 * self.experts), 8)
        self.tiles = self.width // self.depth
        self.extra = -(-(1 + self.experts // 8) // self.tiles) * 8
        self.ride = -(-(CORES * self.experts // 8) // self.tiles) * 8

    def tile(self, g):
        r, q = g // self.tiles * 8, g % self.tiles * self.depth
        return slice(r, r + 8), slice(q, q + self.depth)


def pad_kernel(z, tokens_ref, ids_ref, router_ref, out):
    out[0 : z.toks, :] = tokens_ref[...]
    blank = jnp.zeros((z.extra, z.width), BF16)
    out[z.toks : z.toks + z.extra, :] = blank
    out[z.toks : z.toks + 8, 0 : z.toks] = ids_ref[...].astype(F32).astype(BF16)
    for g in range(z.experts // 8):
        rows, cols = z.tile(g + 1)
        out[z.toks + rows.start : z.toks + rows.stop, cols] = router_ref[8 * g : 8 * g + 8, :]


def served_expert(z, q):
    return lax.axis_index("expert") * z.near + lax.bitwise_xor(lax.axis_index("zero"), q * CORES)


def ids_of(z, block_ref):
    return block_ref[z.toks : z.toks + 8, 0 : z.toks].astype(F32).astype(jnp.int32)


def slot_marks(z, ids_t, offsets):
    has = jnp.concatenate(
        [
            jnp.max((ids_t == served_expert(z, q)).astype(F32), axis=0, keepdims=True)
            for q in offsets
        ]
        * 2,
        axis=0,
    )
    earlier = (
        lax.broadcasted_iota(jnp.int32, (z.toks, z.toks), 0)
        < lax.broadcasted_iota(jnp.int32, (z.toks, z.toks), 1)
    ).astype(F32).astype(BF16)
    slot = jnp.dot(has.astype(BF16), earlier, preferred_element_type=F32)
    slot = jnp.where(has > 0, slot, -1.0)
    row = lax.broadcasted_iota(jnp.int32, (z.cap, z.toks), 0).astype(F32)
    return [jnp.where(row == slot[q : q + 1, :], 1.0, 0.0) for q in range(z.chips)]


def pick_kernel(z, n, offsets, ride, *refs):
    blocks, outs = refs[:n], refs[n:]
    marks = [jnp.concatenate(slot_marks(z, ids_of(z, b), offsets), axis=0).astype(BF16) for b in blocks]
    part = z.width // PARTS
    for c in range(PARTS):
        cols = slice(c * part, (c + 1) * part)
        rows = [jnp.dot(m, b[0 : z.toks, cols], preferred_element_type=F32) for m, b in zip(marks, blocks)]
        for q in range(z.chips):
            mine = [r[q * z.cap : (q + 1) * z.cap] for r in rows]
            outs[q][0 : n * z.cap, cols] = jnp.concatenate(mine, axis=0).astype(BF16)
    if ride:
        for r in range(CORES):
            for g in range(z.experts // 8):
                rows, cols = z.tile(g + 1)
                piece = blocks[r][z.toks + rows.start : z.toks + rows.stop, cols]
                rows, cols = z.tile(r * (z.experts // 8) + g)
                for q in range(z.chips):
                    outs[q][n * z.cap + rows.start : n * z.cap + rows.stop, cols] = piece


def expert_kernel(z, rows, *refs):
    slabs, gate_ref, up_ref, down_ref = refs[: z.chips], *refs[z.chips : z.chips + 3]
    outs, (x, hidden) = refs[z.chips + 3 : 2 * z.chips + 3], refs[2 * z.chips + 3 :]
    for q in range(z.chips):
        x[q * rows : (q + 1) * rows, :] = slabs[q][0:rows, :]
    ff = gate_ref.shape[1]
    tile = ff
    for f in range(0, ff, tile):
        gate = jnp.dot(x[...], gate_ref[:, f : f + tile], preferred_element_type=F32)
        upper = jnp.dot(x[...], up_ref[:, f : f + tile], preferred_element_type=F32)
        hidden[:, f : f + tile] = (gate / (1.0 + jnp.exp(-gate)) * upper).astype(BF16)
    tile = z.width // PARTS
    for c in range(0, z.width, tile):
        y = jnp.dot(hidden[...], down_ref[:, c : c + tile], preferred_element_type=F32)
        for q in range(z.chips):
            outs[q][:, c : c + tile] = y[q * rows : (q + 1) * rows].astype(BF16)


def mix_kernel(z, n, offsets, ride_offsets, *refs):
    blocks, refs = refs[:n], refs[n:]
    riders, backs, outs = refs[: z.chips], refs[z.chips : 2 * z.chips], refs[2 * z.chips :]
    number = lax.broadcasted_iota(jnp.int32, (z.experts, z.toks), 0)
    routers = {}
    for i, q in enumerate(ride_offsets):
        for r in range(CORES):
            base = CORES * z.cap
            pieces = []
            for g in range(z.experts // 8):
                rows, cols = z.tile(r * (z.experts // 8) + g)
                pieces.append(riders[i][base + rows.start : base + rows.stop, cols].astype(F32))
            routers[CORES * q + r] = jnp.concatenate(pieces, axis=0).astype(BF16)
    for b, block in enumerate(blocks):
        ids_t = ids_of(z, block)
        logits = None
        for o in range(z.near):
            start = pl.multiple_of(lax.bitwise_xor(lax.axis_index("zero"), o) * z.depth, z.depth)
            term = lax.dot_general(
                routers[o],
                block[0 : z.toks, pl.ds(start, z.depth)],
                (((1,), (1,)), ((), ())),
                preferred_element_type=F32,
            )
            logits = term if logits is None else logits + term
        chosen = number == ids_t[0:1, :]
        for k in range(1, z.topk):
            chosen = chosen | (number == ids_t[k : k + 1, :])
        weights = jnp.where(chosen, jnp.exp(jnp.where(chosen, logits, 0.0)), 0.0)
        gates = weights / jnp.sum(weights, axis=0, keepdims=True)
        marks = slot_marks(z, ids_t, offsets)
        mix = []
        for mark, q in zip(marks, offsets):
            gate = jnp.sum(jnp.where(number == served_expert(z, q), gates, 0.0), axis=0, keepdims=True)
            mix.append(mark * gate)
        mix = jnp.concatenate(mix, axis=0).astype(BF16)
        part = z.width // PARTS
        for c in range(PARTS):
            cols = slice(c * part, (c + 1) * part)
            own = slice(b * z.cap, (b + 1) * z.cap)
            y = jnp.concatenate([s[:, cols].astype(F32)[own] for s in backs], axis=0).astype(BF16)
            mixed = lax.dot_general(mix, y, (((0,), (0,)), ((), ())), preferred_element_type=F32).astype(BF16)
            if b == 0:
                outs[0][:, cols] = mixed
            else:
                half = z.toks // 2
                outs[1][:, cols] = mixed[0:half]
                outs[2][:, cols] = mixed[half:]


def join_kernel(*refs):
    out = refs[-1]
    half = out.shape[0] // 2
    for i in range(2):
        rows = slice(i * half, (i + 1) * half)
        total = refs[0][rows, :].astype(F32) + refs[1 + i][...].astype(F32)
        for ref in refs[3:-1]:
            total = total + ref[rows, :].astype(F32)
        out[rows, :] = total.astype(BF16)


def per_device(tokens, router_weight, expert_ids, gate_weight, up_weight, down_weight):
    layers, near = lax.axis_size("expert"), lax.axis_size("zero")
    z = Sizes(tokens, router_weight.T, expert_ids.T, near, layers)

    def along(array, d):
        return lax.ppermute(array, "expert", [(i, (i + d) % layers) for i in range(layers)])

    def across(array, o):
        return lax.ppermute(array, "zero", [(i, i ^ o) for i in range(near)]) if o else array

    def after(arrays, *others):
        return list(lax.optimization_barrier((*arrays, *others))[: len(arrays)])

    def shape(rows):
        return jax.ShapeDtypeStruct((rows, z.width), BF16)

    forward = list(range(z.chips))
    backward = [0] + forward[:0:-1]
    out_order = {0: forward, 1: forward[:-2] + forward[:-3:-1]}
    ride_order = out_order[1]

    def pick(blocks, d, flops=1000):
        n = len(blocks)
        offsets = out_order.get(d, backward)
        rows = n * z.cap + (z.ride if d == 1 else 0)
        body = functools.partial(pick_kernel, z, n, offsets, d == 1)
        return dict(zip(offsets, call(body, [shape(rows)] * z.chips, n, flops=flops)(*blocks)))

    def arrived(arrays):
        out = jax.ShapeDtypeStruct((8, 128), BF16)
        return call(arrived_kernel, out, len(arrays), flops=PHASE_FLOPS)(*arrays)

    def slabs_across(slabs):
        return {q: across(s, CORES * q) for q, s in slabs.items()}

    def expert(slabs, *first, flops=1000):
        rows = CORES * z.cap
        offsets = list(slabs)
        outs = call(
            functools.partial(expert_kernel, z, rows),
            [shape(rows)] * z.chips,
            z.chips + 3,
            [
                pltpu.VMEM((z.chips * rows, z.width), BF16),
                pltpu.VMEM((z.chips * rows, gate_weight.shape[2]), BF16),
            ],
            flops,
        )(*after(list(slabs.values()), *first), gate_weight[0], up_weight[0], down_weight[0])
        return dict(zip(offsets, outs))

    def mix(blocks, backs, *first):
        riders = [slots[1][q] for q in ride_order]
        n = len(blocks)
        mine, *other = call(
            functools.partial(mix_kernel, z, n, list(backs), ride_order),
            [shape(z.toks), shape(z.toks // 2), shape(z.toks // 2)],
            n + 2 * z.chips,
            flops=PHASE_FLOPS,
        )(*blocks, *riders, *after(list(backs.values()), *first))
        return [mine] + [across(part, 1) for part in other]

    def join(parts):
        return call(join_kernel, shape(z.toks), len(parts))(*parts)

    own = call(functools.partial(pad_kernel, z), shape(z.toks + z.extra), 3)(
        tokens, expert_ids.T, router_weight.T
    )

    end = layers - 1
    turns = [(d, True) for d in range(end)] + [(d, False) for d in range(1, end)]
    turns += [(end, True), (end, False), (0, False)]
    blocks, pairs, slots, results = {0: own}, {}, {}, {}
    leaving, home, seen, waiting = {}, {}, None, None
    for d, outward in turns:
        if outward:
            if d:
                blocks[d] = after([along(blocks[d - 1], 1)], slots[d - 1][1])[0]
            pairs[d] = [blocks[d], across(blocks[d], 1)]
            rows = slabs = pick(pairs[d], d, PHASE_FLOPS if d == end else 1000)
            if 0 < d < end:
                gate = [slots[d - 1][q] for q in forward[1:]] + ([results[d - 2][0]] if d > 1 else [])
                gate = arrived(gate)
                rows = {q: after([s], gate)[0] for q, s in slabs.items()}
                results[d - 1] = expert(slots[d - 1], slabs[0])
            if d == end:
                rows = {q: after([s], seen[q])[0] for q, s in slabs.items()}
            seen = slots[d] = slabs_across(rows)
            if d == end - 1:
                results[d] = expert(slots[d])
            if d == end:
                first = [leaving[e] for e in range(1, end)]
                results[d] = expert(slots[d], *first, flops=PHASE_FLOPS)
        else:
            rows = {q: after([results[d][q]], seen[q])[0] for q in backward}
            seen = backs = slabs_across(rows)
            first = [(home if d else leaving)[waiting]] if waiting else [results[end - 1][0]]
            sums = mix(pairs[d], backs, *first)
            if d:
                leaving[d] = join(sums)
                home[d] = along(leaving[d], layers - d)
                waiting = d
    return join(sums + [home[d] for d in range(1, layers)])


def solution(mesh):
    everything = ("expert", "zero")
    in_specs = (
        P(everything, None),
        P("zero", None),
        P(everything, None),
        P(everything, None, None),
        P(everything, None, None),
        P(everything, None, None),
    )
    return jax.shard_map(
        per_device, mesh=mesh, in_specs=in_specs, out_specs=P(everything, None), check_vma=False
    )
```
